128 devices in a mesh: node: 32 (over y, x, z_lo), local: 4 (over z_hi, core).
Axes of the slice: x: 4, y: 4, z: 4 (z_hi: 2, z_lo: 2; z = z_hi * 2 + z_lo), core: 2. Of those that a mesh axis runs over, the one named last changes fastest.
Arguments:
- tokens: bfloat16 [16384, 4096], P(('node', 'local')), may hold values from -6 to 6
- grad_out: bfloat16 [16384, 4096], P(('node', 'local')), may hold values from -6 to 6
- router_logits: float32 [16384, 128], P(('node', 'local')), may hold values from -20 to 280
- group_id: int32 [16384], P(('node', 'local')), may hold values from 0 to 15, as said below
- expert_ids: int32 [16384, 2], P(('node', 'local')), may hold values from 0 to 7, as said below
- w_gate: bfloat16 [32, 4096, 1536], P('node', None, 'local'), may hold values from -0.09375 to 0.09375
- w_up: bfloat16 [32, 4096, 1536], P('node', None, 'local'), may hold values from -0.09375 to 0.09375
- w_down: bfloat16 [32, 1536, 4096], P('node', 'local'), may hold values from -0.15625 to 0.15625
Outputs:
- mixed: bfloat16 [16384, 4096], P(('node', 'local'))
- d_tokens: bfloat16 [16384, 4096], P(('node', 'local'))
- d_logits: float32 [16384, 128], P(('node', 'local'))
- grad_gate: bfloat16 [32, 4096, 1536], P('node', None, 'local')
- grad_up: bfloat16 [32, 4096, 1536], P('node', None, 'local')
- grad_down: bfloat16 [32, 1536, 4096], P('node', 'local')
The draws below stay inside these ranges and needn't reach their ends.
Inputs may be any that keep to these rules, and one draw needn't show every extreme that they name: `group_id`: A token is computed here when its group is below 4. Among the tokens of one device no expert of those groups is named by more than 6 tokens, and one such expert is named by exactly 6 tokens of every device. `expert_ids`: the two numbers of a token differ; both name experts of the token's group.
All inputs are finite; a program needn't handle non-finite values.
Results may differ from the reference program's by a relative error of at most 0.0065.
Values may be sent and summed in bfloat16 or wider, within the bound.
No kernel may reach another device: no remote copies, remote signals or barrier semaphores. Data moves between devices by JAX's collectives and lax.ppermute only.
A program may use at most 192 MiB of HBM per device.

```python
import math
import jax
import jax.numpy as jnp
from jax import lax

D = 4096
F = 1536
GSIZE = 8
GROUPS_ALL = 16
LOGITS = 128
EXPERTS = 32
WGROUPS = 4
TOK_DEV = 128
CAP = 6
TOKENS = 16384


def routing_table(key):
    base_key = jax.random.fold_in(key, 7301)
    subkeys = jax.random.split(base_key, 8)
    block_count = TOKENS // TOK_DEV
    window_groups = EXPERTS // GSIZE
    window_pick = jax.random.randint(subkeys[0], (TOKENS,), 0, 2)
    inside_group = jax.random.randint(subkeys[1], (TOKENS,), 0, window_groups)
    outside_group = window_groups + jax.random.randint(subkeys[2], (TOKENS,), 0, GROUPS_ALL - window_groups)
    group_ids = jnp.where(window_pick == 0, inside_group, outside_group)
    first_draw = jax.random.randint(subkeys[3], (TOKENS,), 0, GSIZE)
    second_draw = jax.random.randint(subkeys[4], (TOKENS,), 0, GSIZE)
    relabel = jax.random.permutation(subkeys[5], GSIZE)
    first_expert = relabel[jnp.minimum(first_draw, second_draw)]
    offset_draw = jax.random.randint(subkeys[6], (TOKENS,), 1, GSIZE)
    hot_expert = jax.random.randint(subkeys[7], (), 0, EXPERTS)
    block_keys = jax.random.split(jax.random.fold_in(base_key, 11), block_count)
    block_ranks = jax.vmap(lambda single: jax.random.permutation(single, TOK_DEV))(block_keys)
    forced = (block_ranks < CAP).reshape(TOKENS)
    group_ids = jnp.where(forced, hot_expert // GSIZE, group_ids)
    first_expert = jnp.where(forced, hot_expert % GSIZE, first_expert)
    second_expert = (first_expert + offset_draw) % GSIZE
    pair_ids = jnp.stack([first_expert, second_expert], axis=1)
    inside = group_ids < window_groups
    target = jnp.where(inside[:, None], group_ids[:, None] * GSIZE + pair_ids, EXPERTS)
    expert_range = jnp.arange(EXPERTS, dtype=jnp.int32)
    onehot = (target[:, :, None] == expert_range[None, None, :]).astype(jnp.int32)
    per_token = jnp.sum(onehot, axis=1).reshape(block_count, TOK_DEV, EXPERTS)
    positions = jnp.arange(TOK_DEV, dtype=jnp.int32)[None, :]
    order_key = jnp.where(forced.reshape(block_count, TOK_DEV), 0, TOK_DEV) + positions
    order_index = jnp.argsort(order_key, axis=1, stable=True)
    ordered = jnp.take_along_axis(per_token, order_index[:, :, None], axis=1)
    earlier = jnp.cumsum(ordered, axis=1) - ordered
    inverse = jnp.argsort(order_index, axis=1, stable=True)
    rank_table = jnp.take_along_axis(earlier, inverse[:, :, None], axis=1).reshape(TOKENS, 1, EXPERTS)
    slot_rank = jnp.sum(onehot * rank_table, axis=2)
    over_cap = jnp.any(inside[:, None] & (slot_rank >= CAP), axis=1)
    group_ids = jnp.where(over_cap, outside_group, group_ids)
    return (group_ids.astype(jnp.int32), pair_ids.astype(jnp.int32))


def draw_group_id(key, part):
    return routing_table(key)[0]


def draw_expert_ids(key, part):
    return routing_table(key)[1]


def draw_router_logits(key, part):
    base_key = jax.random.fold_in(key, 4409)
    subkeys = jax.random.split(base_key, 6)
    group_ids = routing_table(key)[0]
    columns = jnp.arange(LOGITS, dtype=jnp.int32)
    member = (columns // GSIZE)[None, :] == group_ids[:, None]
    depth = jax.random.uniform(subkeys[5], (TOKENS, 1), jnp.float32, 9.0, 10.0)
    lowered = jnp.where(member, depth, 0.0)
    column_scale = jnp.exp(jax.random.uniform(subkeys[0], (LOGITS,), jnp.float32, math.log(0.5), math.log(0.8)))
    base_values = jnp.clip(jax.random.normal(subkeys[2], (TOKENS, LOGITS), jnp.float32) * column_scale[None, :], -12.0, 12.0)
    values = jnp.clip(base_values - lowered, -20.0, 20.0)
    return values.astype(jnp.float32)


def block_levels(own_key, dims, shards, smallest, high):
    def one(dim, parts):
        draws = jax.random.uniform(jax.random.fold_in(jax.random.fold_in(own_key, 6), dim), (parts,), jnp.float32, smallest / len(shards), high / len(shards))
        return jnp.repeat(jnp.exp(draws), dims[dim] // parts).reshape((-1,) + (1,) * (len(dims) - dim - 1))

    loudness = one(*shards[0])
    for cut in shards[1:]:
        loudness = loudness * one(*cut)
    return loudness


def scatter_about(key, shape, scale, reach, cuts=(), kind=jnp.bfloat16):
    array = scale * jax.random.normal(key, shape, jnp.float32)
    if cuts:
        array = array * block_levels(key, shape, cuts, -0.22, 0.18)
    return jnp.clip(array, -reach, reach).astype(kind)


def setup_inputs(seed: int = 0) -> dict:
    keys = jax.random.split(jax.random.key(seed), 9)
    tokens = scatter_about(keys[0], (TOKENS, D), 1.0, 6.0, ((0, 128),))
    grad_out = scatter_about(keys[1], (TOKENS, D), 1.0, 6.0, ((0, 128),))
    router_logits = draw_router_logits(jax.random.fold_in(keys[8], 71), 0)
    group_id = draw_group_id(jax.random.fold_in(keys[8], 71), 0)
    expert_ids = draw_expert_ids(jax.random.fold_in(keys[8], 71), 0)
    w_gate = scatter_about(keys[5], (EXPERTS, D, F), D ** -0.5, 0.09375, ((0, 32), (2, 4)))
    w_up = scatter_about(keys[6], (EXPERTS, D, F), D ** -0.5, 0.09375, ((0, 32), (2, 4)))
    w_down = scatter_about(keys[7], (EXPERTS, F, D), F ** -0.5, 0.15625, ((0, 32), (1, 4)))
    return dict(tokens=tokens, grad_out=grad_out, router_logits=router_logits, group_id=group_id, expert_ids=expert_ids, w_gate=w_gate, w_up=w_up, w_down=w_down)


def gate_weights(logits, group_ids, chosen, inside):
    probabilities = jax.nn.softmax(logits, axis=-1)
    columns = jnp.arange(logits.shape[1], dtype=jnp.int32)
    member = ((columns // GSIZE)[None, :] == group_ids[:, None]).astype(logits.dtype)
    group_mass = lax.optimization_barrier(jnp.sum(probabilities * member, axis=1))
    picked = lax.optimization_barrier(jnp.sum(jnp.where(chosen[:, :, None] == columns[None, None, :], logits[:, None, :], 0.0), axis=2))
    pair_share = jax.nn.softmax(picked, axis=-1)
    return jnp.where(inside[:, None], group_mass[:, None] * pair_share, 0.0)

def expert_pass(operands):
    rows_in, grads_in, gate_matrix, up_matrix, down_matrix = operands
    gate_pre = jnp.dot(rows_in, gate_matrix, preferred_element_type=jnp.float32)
    up_pre = jnp.dot(rows_in, up_matrix, preferred_element_type=jnp.float32)
    sigmoid_gate = jax.nn.sigmoid(gate_pre)
    activated = gate_pre * sigmoid_gate
    hidden = (activated * up_pre).astype(jnp.bfloat16)
    expert_out = jnp.dot(hidden, down_matrix, preferred_element_type=jnp.float32).astype(jnp.bfloat16)
    grad_hidden = jnp.dot(grads_in, down_matrix.T, preferred_element_type=jnp.float32)
    grad_gate_pre = (grad_hidden * up_pre * sigmoid_gate * (1.0 + gate_pre * (1.0 - sigmoid_gate))).astype(jnp.bfloat16)
    grad_up_pre = (grad_hidden * activated).astype(jnp.bfloat16)
    expert_back = (jnp.dot(grad_gate_pre, gate_matrix.T, preferred_element_type=jnp.float32) + jnp.dot(grad_up_pre, up_matrix.T, preferred_element_type=jnp.float32)).astype(jnp.bfloat16)
    gate_grad = jnp.dot(rows_in.T, grad_gate_pre, preferred_element_type=jnp.float32).astype(jnp.bfloat16)
    up_grad = jnp.dot(rows_in.T, grad_up_pre, preferred_element_type=jnp.float32).astype(jnp.bfloat16)
    down_grad = jnp.dot(hidden.T, grads_in, preferred_element_type=jnp.float32).astype(jnp.bfloat16)
    return (expert_out, expert_back, gate_grad, up_grad, down_grad)

def reference(tokens, grad_out, router_logits, group_id, expert_ids, w_gate, w_up, w_down):
    block_count = TOKENS // TOK_DEV
    inside = group_id < WGROUPS
    chosen = group_id[:, None] * GSIZE + expert_ids
    target = jnp.where(inside[:, None], chosen, EXPERTS)
    expert_range = jnp.arange(EXPERTS, dtype=jnp.int32)
    onehot = (target[:, :, None] == expert_range[None, None, :]).astype(jnp.int32)
    per_token = lax.optimization_barrier(jnp.sum(onehot, axis=1)).reshape(block_count, TOK_DEV, EXPERTS)
    earlier = (jnp.cumsum(per_token, axis=1) - per_token).reshape(TOKENS, 1, EXPERTS)
    slot_rank = lax.optimization_barrier(jnp.sum(onehot * earlier, axis=2))
    block_of = (jnp.arange(TOKENS, dtype=jnp.int32) // TOK_DEV)[:, None]
    slot_total = EXPERTS * block_count * CAP
    position = jnp.where(inside[:, None], (target * block_count + block_of) * CAP + slot_rank, slot_total).astype(jnp.int32)
    flat_position = position.reshape(-1)
    assignment_range = jnp.arange(2 * TOKENS, dtype=jnp.int32)
    assign_of = jnp.zeros((slot_total + 1,), jnp.int32).at[flat_position].set(assignment_range)
    filled = jnp.zeros((slot_total + 1,), jnp.int32).at[flat_position].set(1)
    filled = filled[:slot_total] > 0
    assign_used = assign_of[:slot_total]
    mix_weights, pull_back = jax.vjp(lambda values: gate_weights(values, group_id, chosen, inside), router_logits)
    grad_f32 = grad_out.astype(jnp.float32)
    weighted_grad = (mix_weights[:, :, None] * grad_f32[:, None, :]).astype(jnp.bfloat16).reshape(2 * TOKENS, D)
    token_rows = tokens[assign_used // 2]
    rows_buffer = jnp.where(filled[:, None], token_rows, jnp.zeros_like(token_rows)).reshape(EXPERTS, block_count * CAP, D)
    grad_rows = weighted_grad[assign_used]
    grads_buffer = jnp.where(filled[:, None], grad_rows, jnp.zeros_like(grad_rows)).reshape(EXPERTS, block_count * CAP, D)
    expert_out, expert_back, grad_gate, grad_up, grad_down = lax.map(expert_pass, (rows_buffer, grads_buffer, w_gate, w_up, w_down))
    out_flat = jnp.concatenate([expert_out.reshape(slot_total, D), jnp.zeros((1, D), expert_out.dtype)], axis=0)
    back_flat = jnp.concatenate([expert_back.reshape(slot_total, D), jnp.zeros((1, D), expert_back.dtype)], axis=0)
    out_rows = out_flat[position].astype(jnp.float32)
    back_rows = back_flat[position].astype(jnp.float32)
    mixed = lax.optimization_barrier(jnp.sum(mix_weights[:, :, None] * out_rows, axis=1)).astype(jnp.bfloat16)
    d_tokens = lax.optimization_barrier(jnp.sum(back_rows, axis=1)).astype(jnp.bfloat16)
    scores = lax.optimization_barrier(jnp.sum(grad_f32[:, None, :] * out_rows, axis=2))
    d_logits = pull_back(scores)[0]
    return (mixed, d_tokens, d_logits, grad_gate, grad_up, grad_down)
```

```python
import jax
import jax.numpy as jnp
from jax import lax
from jax.sharding import Mesh, PartitionSpec as P

GSIZE = 8
CAP = 6
CUT = 4
TEAM = 8
WIDE = ("y", "x", "l", "h")
ALL = ("y", "x", "l", "h", "c")
NODE = ("y", "x", "l")
LOCAL = ("h", "c")
F32 = jnp.float32
BF16 = jnp.bfloat16


def dot(a, b, dims=((1,), (0,))):
    return lax.dot_general(a, b, (dims, ((), ())), preferred_element_type=F32)


def gate_weights(logits, group_ids, chosen, inside):
    probabilities = jax.nn.softmax(logits, axis=-1)
    columns = jnp.arange(logits.shape[1], dtype=jnp.int32)
    member = ((columns // GSIZE)[None, :] == group_ids[:, None]).astype(logits.dtype)
    group_mass = jnp.sum(probabilities * member, axis=1)
    picked = jnp.sum(
        jnp.where(chosen[:, :, None] == columns[None, None, :], logits[:, None, :], 0.0), axis=2
    )
    pair_share = jax.nn.softmax(picked, axis=-1)
    return jnp.where(inside[:, None], group_mass[:, None] * pair_share, 0.0)


def exchange(value):
    return lax.all_to_all(value, WIDE, split_axis=0, concat_axis=0, tiled=True)


def swap(value):
    return lax.ppermute(value, "c", [(0, 1), (1, 0)])


def order_matrix():
    wanted = jnp.arange(TEAM * CUT * CAP, dtype=jnp.int32)
    chunk, source, slot = wanted // (TEAM * CAP), wanted // CAP % TEAM, wanted % CAP
    held = (source * CUT + chunk) * CAP + slot
    return (held[:, None] == wanted[None, :]).astype(BF16)


def to_rows(blocks, order):
    peers, lines, width = blocks.shape
    teams = peers // TEAM
    held = blocks.reshape(teams, TEAM * lines, width)
    moved = jnp.einsum("pq,gqc->gpc", order, held, preferred_element_type=F32).astype(BF16)
    moved = moved.reshape(teams, CUT, TEAM * CAP, width)
    return moved.transpose(0, 2, 1, 3).reshape(peers * CAP, CUT * width)


def to_blocks(rows, order):
    count, model_width = rows.shape
    peers, width = count // CAP, model_width // CUT
    teams = peers // TEAM
    held = rows.reshape(teams, TEAM * CAP, CUT, width).transpose(0, 2, 1, 3)
    held = held.reshape(teams, CUT * TEAM * CAP, width)
    moved = jnp.einsum("pq,gpc->gqc", order, held, preferred_element_type=F32).astype(BF16)
    return moved.reshape(peers, CUT * CAP, width)


def body(tokens, grad_out, router_logits, group_id, expert_ids, w_gate, w_up, w_down):
    w_gate, w_up, w_down = w_gate[0], w_up[0], w_down[0]
    count, model_width = tokens.shape
    width = model_width // CUT
    expert_total = lax.axis_size(NODE)
    sides = lax.axis_size("h")
    peers = expert_total * sides
    inside = group_id < expert_total // GSIZE
    chosen = group_id[:, None] * GSIZE + expert_ids
    target = jnp.where(inside[:, None], chosen, expert_total)
    expert_range = jnp.arange(expert_total, dtype=jnp.int32)
    onehot = (target[:, :, None] == expert_range[None, None, :]).astype(F32)
    per_token = jnp.sum(onehot, axis=1)
    position = jnp.arange(count, dtype=jnp.int32)
    before = (position[:, None] > position[None, :]).astype(BF16)
    earlier = dot(before, per_token.astype(BF16))
    rank = jnp.sum(onehot * earlier[:, None, :], axis=2).astype(jnp.int32)
    slot = jnp.where(inside[:, None], target * CAP + rank, -1)
    line = jnp.arange(peers * CUT * CAP, dtype=jnp.int32)
    line_slot = line // (CUT * CAP) // sides * CAP + line % CAP
    line_key = line_slot * CUT + line // CAP % CUT
    chunk = jnp.arange(CUT, dtype=jnp.int32)
    token_key = jnp.where(
        slot[None] >= 0, slot[None] * CUT + chunk[:, None, None], -1
    ).reshape(CUT * count, 2)
    first = line_key[:, None] == token_key[None, :, 0]
    second = line_key[:, None] == token_key[None, :, 1]
    either = (first | second).astype(BF16)
    first, second = first.astype(BF16), second.astype(BF16)
    mix_weights, pull_back = jax.vjp(
        lambda values: gate_weights(values, group_id, chosen, inside), router_logits
    )

    def stacked(rows):
        return rows.reshape(count, CUT, width).transpose(1, 0, 2).reshape(CUT * count, width)

    def flat(rows):
        return rows.reshape(CUT, count, width).transpose(1, 0, 2).reshape(count, model_width)

    order = order_matrix()
    block = (peers, CUT * CAP, width)
    tokens_out = dot(either, stacked(tokens)).astype(BF16).reshape(block)
    line_weight = jnp.sum(
        jnp.where(line_slot[:, None] == slot[None, :, 0], mix_weights[None, :, 0], 0.0)
        + jnp.where(line_slot[:, None] == slot[None, :, 1], mix_weights[None, :, 1], 0.0),
        axis=1,
    )
    grads_out = (dot(either, stacked(grad_out)) * line_weight[:, None]).astype(BF16).reshape(block)

    tokens_in, grads_out = lax.optimization_barrier((exchange(tokens_out), grads_out))
    grads_in = exchange(grads_out)
    rows_own = to_rows(tokens_in, order)
    half = rows_own.shape[0]
    rows = jnp.concatenate([rows_own, swap(rows_own)], axis=0)
    gate_pre = dot(rows, w_gate)
    up_pre = dot(rows, w_up)
    sigmoid_gate = jax.nn.sigmoid(gate_pre)
    activated = gate_pre * sigmoid_gate
    hidden = (activated * up_pre).astype(BF16)
    out_other = dot(hidden[half:], w_down).astype(BF16)
    out_sum = (dot(hidden[:half], w_down) + swap(out_other).astype(F32)).astype(BF16)
    out_blocks, grads_in = lax.optimization_barrier((to_blocks(out_sum, order), grads_in))
    out_back = exchange(out_blocks)

    grads_own = to_rows(grads_in, order)
    grads = jnp.concatenate([grads_own, swap(grads_own)], axis=0)
    grad_hidden = dot(grads, w_down, ((1,), (1,)))
    grad_gate_pre = (
        grad_hidden * up_pre * sigmoid_gate * (1.0 + gate_pre * (1.0 - sigmoid_gate))
    ).astype(BF16)
    grad_up_pre = (grad_hidden * activated).astype(BF16)

    def back(part):
        return dot(grad_gate_pre[part], w_gate, ((1,), (1,))) + dot(
            grad_up_pre[part], w_up, ((1,), (1,))
        )

    in_other = back(slice(half, None)).astype(BF16)
    in_sum = (back(slice(0, half)) + swap(in_other).astype(F32)).astype(BF16)
    in_blocks, out_back = lax.optimization_barrier((to_blocks(in_sum, order), out_back))
    in_back = exchange(in_blocks).reshape(-1, width)
    out_back = out_back.reshape(-1, width)

    in_blocks, rows, hidden, grads, grad_gate_pre, grad_up_pre = lax.optimization_barrier(
        (in_blocks, rows, hidden, grads, grad_gate_pre, grad_up_pre)
    )
    grad_gate = dot(rows, grad_gate_pre, ((0,), (0,))).astype(BF16)
    grad_up = dot(rows, grad_up_pre, ((0,), (0,))).astype(BF16)
    grad_down = dot(hidden, grads, ((0,), (0,))).astype(BF16)

    first_out = flat(dot(first, out_back, ((0,), (0,))))
    second_out = flat(dot(second, out_back, ((0,), (0,))))
    grad_f32 = grad_out.astype(F32)
    mixed = (mix_weights[:, 0:1] * first_out + mix_weights[:, 1:2] * second_out).astype(BF16)
    scores = jnp.stack(
        [jnp.sum(grad_f32 * first_out, axis=1), jnp.sum(grad_f32 * second_out, axis=1)], axis=1
    )
    d_logits = pull_back(scores)[0]
    d_tokens = flat(dot(either, in_back, ((0,), (0,)))).astype(BF16)
    return (mixed, d_tokens, d_logits, grad_gate[None], grad_up[None], grad_down[None])


def solution(mesh):
    fine = Mesh(mesh.devices.reshape(4, 4, 2, 2, 2), ALL)
    return jax.shard_map(
        body,
        mesh=fine,
        in_specs=(
            P(ALL, None),
            P(ALL, None),
            P(ALL, None),
            P(ALL),
            P(ALL, None),
            P(NODE, None, LOCAL),
            P(NODE, None, LOCAL),
            P(NODE, LOCAL, None),
        ),
        out_specs=(
            P(ALL, None),
            P(ALL, None),
            P(ALL, None),
            P(NODE, None, LOCAL),
            P(NODE, None, LOCAL),
            P(NODE, LOCAL, None),
        ),
        check_vma=False,
    )
```

```python
import functools

import jax
import jax.numpy as jnp
import numpy as np
from jax import lax
from jax.experimental import pallas as pl
from jax.experimental.pallas import tpu as pltpu
from jax.sharding import Mesh, PartitionSpec as P

GSIZE = 8
CAP = 6
CUT = 4
TEAM = 8
LINES = CUT * CAP
BUSY = 200_000_000_000
WIDE = ("y", "x", "l", "h")
ALL = ("y", "x", "l", "h", "c")
NODE = ("y", "x", "l")
LOCAL = ("h", "c")
F32 = jnp.float32
BF16 = jnp.bfloat16


def dot(a, b, dims=((1,), (0,))):
    return lax.dot_general(a, b, (dims, ((), ())), preferred_element_type=F32)


def across(a, b):
    return dot(a, b, ((1,), (1,)))


def call(kernel, name, outs, flops=1, **more):
    return pl.pallas_call(
        kernel,
        out_shape=outs,
        name=name,
        cost_estimate=pl.CostEstimate(flops=flops, bytes_accessed=1, transcendentals=0),
        compiler_params=pltpu.CompilerParams(vmem_limit_bytes=52 << 20),
        **more,
    )


def whole(shape):
    return pl.BlockSpec(shape, lambda *_: (0,) * len(shape))


def gate_weights(logits, group_ids, chosen, inside):
    probabilities = jax.nn.softmax(logits, axis=-1)
    columns = jnp.arange(logits.shape[1], dtype=jnp.int32)
    member = ((columns // GSIZE)[None, :] == group_ids[:, None]).astype(logits.dtype)
    group_mass = jnp.sum(probabilities * member, axis=1)
    picked = jnp.sum(
        jnp.where(chosen[:, :, None] == columns[None, None, :], logits[:, None, :], 0.0), axis=2
    )
    pair_share = jax.nn.softmax(picked, axis=-1)
    return jnp.where(inside[:, None], group_mass[:, None] * pair_share, 0.0)


def exchange(value):
    blocks = value.reshape(-1, LINES, value.shape[-1])
    out = lax.all_to_all(blocks, WIDE, split_axis=0, concat_axis=0, tiled=True)
    return out.reshape(value.shape)


def swap(value):
    return lax.ppermute(value, "c", [(0, 1), (1, 0)])


def order_matrix(copies):
    line = np.arange(TEAM * copies * LINES)
    member, chunk, slot = line // (copies * LINES), line // CAP % CUT, line % CAP
    wanted = (chunk * TEAM + member) * CAP + slot
    return (wanted[:, None] == np.arange(TEAM * LINES)[None, :]).astype(BF16)


def gathered(ref, start, width):
    team = pl.ds(start, TEAM * CAP)
    return jnp.concatenate([ref[team, j * width : (j + 1) * width] for j in range(CUT)], axis=0)


def slots_kernel(expert_total, group_ref, expert_ref, rows_ref, spread_ref, out_ref, slot_ref, held):
    team = pl.program_id(0)
    width = out_ref.shape[1]

    @pl.when(team == 0)
    def _():
        count = group_ref.shape[1]
        group = group_ref[...]
        inside = group < expert_total // GSIZE
        down = lax.broadcasted_iota(jnp.int32, (count, count), 0)
        along = lax.broadcasted_iota(jnp.int32, (count, count), 1)
        expert = lax.broadcasted_iota(jnp.int32, (expert_total, count), 0)
        targets, hots = [], []
        for k in range(2):
            column = expert_ref[:, k : k + 1].astype(F32)
            row = jnp.sum(jnp.where(down == along, column, 0.0), axis=0, keepdims=True)
            target = jnp.where(inside, group * GSIZE + row.astype(jnp.int32), expert_total)
            targets.append(target)
            hots.append((expert == target).astype(F32))
        before = (down < along).astype(F32).astype(BF16)
        earlier = dot((hots[0] + hots[1]).astype(BF16), before)
        place = lax.broadcasted_iota(jnp.int32, (expert_total * CAP, count), 0)
        picked = None
        for k in range(2):
            rank = jnp.sum(hots[k] * earlier, axis=0, keepdims=True).astype(jnp.int32)
            slot = jnp.where(inside, targets[k] * CAP + rank, -1)
            slot_ref[k : k + 1, :] = slot
            match = place == slot
            picked = match if picked is None else picked | match
        picked = picked.astype(F32).astype(BF16)
        held[...] = dot(picked, rows_ref[...]).astype(BF16)

    start = pl.multiple_of(team * (TEAM * CAP), 16)
    out_ref[...] = dot(spread_ref[...], gathered(held, start, width)).astype(BF16)


def pack_tokens(group_id, expert_ids, tokens, spread, expert_total):
    count, model_width = tokens.shape
    width = model_width // CUT
    teams, lines = expert_total // TEAM, spread.shape[0]
    return call(
        functools.partial(slots_kernel, expert_total),
        "pack_tokens",
        (
            jax.ShapeDtypeStruct((teams * lines, width), BF16),
            jax.ShapeDtypeStruct((2, count), jnp.int32),
        ),
        grid=(teams,),
        in_specs=[
            whole((1, count)),
            whole(expert_ids.shape),
            whole(tokens.shape),
            whole(spread.shape),
        ],
        out_specs=(pl.BlockSpec((lines, width), lambda t: (t, 0)), whole((2, count))),
        scratch_shapes=[pltpu.VMEM((expert_total * CAP, model_width), BF16)],
    )(group_id[None], expert_ids, tokens, spread)


def grads_kernel(slot_ref, weight_ref, rows_ref, spread_ref, out_ref, held):
    team = pl.program_id(0)
    width = out_ref.shape[1]

    @pl.when(team == 0)
    def _():
        place = lax.broadcasted_iota(jnp.int32, (held.shape[0], slot_ref.shape[1]), 0)
        first, second = place == slot_ref[0:1, :], place == slot_ref[1:2, :]
        weight = jnp.where(first, weight_ref[0:1, :], 0.0)
        weight += jnp.where(second, weight_ref[1:2, :], 0.0)
        weight = jnp.sum(weight, axis=1, keepdims=True)
        picked = (first | second).astype(F32).astype(BF16)
        held[...] = (dot(picked, rows_ref[...]) * weight).astype(BF16)

    start = pl.multiple_of(team * (TEAM * CAP), 16)
    out_ref[...] = dot(spread_ref[...], gathered(held, start, width)).astype(BF16)


def pack_grads(slot, weights, grad_out, spread, expert_total):
    count, model_width = grad_out.shape
    width = model_width // CUT
    teams, lines = expert_total // TEAM, spread.shape[0]
    return call(
        grads_kernel,
        "pack_grads",
        jax.ShapeDtypeStruct((teams * lines, width), BF16),
        grid=(teams,),
        in_specs=[
            whole((2, count)),
            whole((2, count)),
            whole(grad_out.shape),
            whole(spread.shape),
        ],
        out_specs=pl.BlockSpec((lines, width), lambda t: (t, 0)),
        scratch_shapes=[pltpu.VMEM((expert_total * CAP, model_width), BF16)],
    )(slot, weights, grad_out, spread)


def put_in_order(lines_ref, order_ref, rows_ref):
    width = lines_ref.shape[1]
    step, rows = TEAM * LINES, TEAM * CAP
    for t in range(lines_ref.shape[0] // step):
        moved = dot(order_ref[...], lines_ref[t * step : (t + 1) * step]).astype(BF16)
        for j in range(CUT):
            columns = slice(j * width, (j + 1) * width)
            rows_ref[t * rows : (t + 1) * rows, columns] = moved[j * rows : (j + 1) * rows]


def forward_kernel(
    lines_ref, order_ref, gate_ref, up_ref, down_ref, rows_ref, g_ref, u_ref, hidden_ref, *out_ref
):
    step = pl.program_id(0)
    width = lines_ref.shape[1]

    @pl.when(step == 0)
    def _():
        put_in_order(lines_ref, order_ref, rows_ref)
        g_ref[...] = jnp.zeros_like(g_ref)
        u_ref[...] = jnp.zeros_like(u_ref)

    rows = rows_ref[:, pl.ds(pl.multiple_of(step * width, width), width)]
    g_ref[...] += dot(rows, gate_ref[...])
    u_ref[...] += dot(rows, up_ref[...])

    @pl.when(step == pl.num_programs(0) - 1)
    def _():
        gate = g_ref[...]
        hidden = (gate * jax.nn.sigmoid(gate) * u_ref[...]).astype(BF16)
        hidden_ref[...] = hidden
        for ref in out_ref:
            for j in range(CUT):
                part = slice(j * width, (j + 1) * width)
                ref[:, part] = dot(hidden, down_ref[:, part]).astype(BF16)


def forward(lines, order, w_gate, w_up, w_down, own):
    width = lines.shape[1]
    half, model_width = lines.shape[0] // CUT, CUT * width
    units = w_down.shape[1]
    wide = jax.ShapeDtypeStruct((half, model_width), BF16)
    weight_spec = pl.BlockSpec((None, width, units), lambda k: (0, k, 0))
    act = whole((half, units))
    outs = [wide] + [jax.ShapeDtypeStruct((half, units), t) for t in (F32, F32, BF16)]
    if not own:
        outs.append(wide)
    down_shape = (None, units, model_width if not own else width)
    return call(
        forward_kernel,
        "forward_own" if own else "forward_other",
        outs,
        BUSY,
        grid=(CUT,),
        in_specs=[
            whole(lines.shape),
            whole(order.shape),
            weight_spec,
            weight_spec,
            pl.BlockSpec(down_shape, lambda k: (0, 0, 0)),
        ],
        out_specs=[whole(wide.shape), act, act, act, whole(wide.shape)][: len(outs)],
    )(lines, order, w_gate, w_up, w_down)


def backward_kernel(
    lines_ref, order_ref, down_ref, g_ref, u_ref, gate_ref, up_ref, rows_ref, dg_ref, du_ref, *more
):
    step = pl.program_id(0)
    width = lines_ref.shape[1]
    *out_ref, total = more

    @pl.when(step == 0)
    def _():
        put_in_order(lines_ref, order_ref, rows_ref)
        total[...] = jnp.zeros_like(total)

    rows = rows_ref[:, pl.ds(pl.multiple_of(step * width, width), width)]
    total[...] += across(rows, down_ref[...])

    @pl.when(step == pl.num_programs(0) - 1)
    def _():
        gate, grad_hidden = g_ref[...], total[...]
        sigmoid_gate = jax.nn.sigmoid(gate)
        dg = grad_hidden * u_ref[...] * sigmoid_gate * (1.0 + gate * (1.0 - sigmoid_gate))
        dg = dg.astype(BF16)
        du = (grad_hidden * (gate * sigmoid_gate)).astype(BF16)
        dg_ref[...] = dg
        du_ref[...] = du
        for ref in out_ref:
            for j in range(CUT):
                part = slice(j * width, (j + 1) * width)
                ref[:, part] = (
                    across(dg, gate_ref[part, :]) + across(du, up_ref[part, :])
                ).astype(BF16)


def backward(lines, order, w_down, gate_pre, up_pre, w_gate, w_up, own):
    width = lines.shape[1]
    half, model_width = lines.shape[0] // CUT, CUT * width
    units = w_down.shape[1]
    wide = jax.ShapeDtypeStruct((half, model_width), BF16)
    weight_shape = (None, model_width if not own else units, units)
    weight_spec = pl.BlockSpec(weight_shape, lambda k: (0, 0, 0))
    act = whole((half, units))
    outs = [wide] + [jax.ShapeDtypeStruct((half, units), BF16)] * 2
    if not own:
        outs.append(wide)
    return call(
        backward_kernel,
        "backward_own" if own else "backward_other",
        outs,
        BUSY,
        grid=(CUT,),
        in_specs=[
            whole(lines.shape),
            whole(order.shape),
            pl.BlockSpec((None, units, width), lambda k: (0, 0, k)),
            act,
            act,
            weight_spec,
            weight_spec,
        ],
        out_specs=[whole(wide.shape), act, act, whole(wide.shape)][: len(outs)],
        scratch_shapes=[pltpu.VMEM((half, units), F32)],
    )(lines, order, w_down, gate_pre, up_pre, w_gate, w_up)


def out_kernel(hidden_ref, down_ref, total_ref):
    total_ref[...] = dot(hidden_ref[...], down_ref[...])


def product_out(hidden, w_down):
    half, units = hidden.shape
    model_width = w_down.shape[2]
    width = model_width // CUT
    return call(
        out_kernel,
        "product_out",
        jax.ShapeDtypeStruct((half, model_width), F32),
        BUSY,
        grid=(CUT,),
        in_specs=[
            whole((half, units)),
            pl.BlockSpec((None, units, width), lambda k: (0, 0, k)),
        ],
        out_specs=pl.BlockSpec((half, width), lambda k: (0, k)),
    )(hidden, w_down)


def in_kernel(dg_ref, du_ref, gate_ref, up_ref, total_ref):
    total_ref[...] = across(dg_ref[...], gate_ref[...]) + across(du_ref[...], up_ref[...])


def product_in(dg, du, w_gate, w_up):
    half, units = dg.shape
    model_width = w_gate.shape[1]
    width = model_width // CUT
    weight_spec = pl.BlockSpec((None, width, units), lambda k: (0, k, 0))
    return call(
        in_kernel,
        "product_in",
        jax.ShapeDtypeStruct((half, model_width), F32),
        BUSY,
        grid=(CUT,),
        in_specs=[whole((half, units)), whole((half, units)), weight_spec, weight_spec],
        out_specs=pl.BlockSpec((half, width), lambda k: (0, k)),
    )(dg, du, w_gate, w_up)


def lines_kernel(total_ref, arrived_ref, order_ref, out_ref):
    width = out_ref.shape[1]
    rows, step = TEAM * CAP, TEAM * LINES
    for t in range(total_ref.shape[0] // rows):
        team = slice(t * rows, (t + 1) * rows)
        pieces = []
        for j in range(CUT):
            part = slice(j * width, (j + 1) * width)
            pieces.append((total_ref[team, part] + arrived_ref[team, part].astype(F32)).astype(BF16))
        held = jnp.concatenate(pieces, axis=0)
        out_ref[t * step : (t + 1) * step, :] = dot(order_ref[...], held).astype(BF16)


def to_lines(total, arrived, order):
    half, model_width = total.shape
    width = model_width // CUT
    parts = 4
    rows = half // parts
    return call(
        lines_kernel,
        "to_lines",
        jax.ShapeDtypeStruct((half * CUT, width), BF16),
        grid=(parts,),
        in_specs=[
            pl.BlockSpec((rows, model_width), lambda k: (k, 0)),
            pl.BlockSpec((rows, model_width), lambda k: (k, 0)),
            whole(order.shape),
        ],
        out_specs=pl.BlockSpec((rows * CUT, width), lambda k: (k, 0)),
    )(total, arrived, order)


def mix_kernel(first_ref, second_ref, lines_ref, grad_ref, weight_ref, mixed_ref, score_ref):
    step = pl.program_id(0)
    count, piece = grad_ref.shape[0], lines_ref.shape[1]
    width = grad_ref.shape[1] // CUT

    @pl.when(step == 0)
    def _():
        score_ref[...] = jnp.zeros_like(score_ref)

    first = dot(first_ref[...], lines_ref[...])
    second = dot(second_ref[...], lines_ref[...])
    for j in range(CUT):
        rows = slice(j * count, (j + 1) * count)
        columns = pl.ds(pl.multiple_of(j * width + step * piece, piece), piece)
        grad = grad_ref[:, columns].astype(F32)
        mixed_ref[:, columns] = (
            weight_ref[:, 0:1] * first[rows] + weight_ref[:, 1:2] * second[rows]
        ).astype(BF16)
        score_ref[:, 0:1] += jnp.sum(grad * first[rows], axis=1, keepdims=True)
        score_ref[:, 1:2] += jnp.sum(grad * second[rows], axis=1, keepdims=True)


def mix(first, second, lines, grad_out, weights):
    total, width = lines.shape
    piece = width // CUT
    return call(
        mix_kernel,
        "mix",
        (
            jax.ShapeDtypeStruct(grad_out.shape, BF16),
            jax.ShapeDtypeStruct(weights.shape, F32),
        ),
        grid=(CUT,),
        in_specs=[
            whole(first.shape),
            whole(second.shape),
            pl.BlockSpec((total, piece), lambda n: (0, n)),
            whole(grad_out.shape),
            whole(weights.shape),
        ],
        out_specs=(whole(grad_out.shape), whole(weights.shape)),
    )(first, second, lines, grad_out, weights)


def unpack_kernel(either_ref, lines_ref, out_ref):
    step = pl.program_id(0)
    count, piece = out_ref.shape[0], lines_ref.shape[1]
    width = out_ref.shape[1] // CUT
    rows = dot(either_ref[...], lines_ref[...]).astype(BF16)
    for j in range(CUT):
        columns = pl.ds(pl.multiple_of(j * width + step * piece, piece), piece)
        out_ref[:, columns] = rows[j * count : (j + 1) * count]


def unpack(either, lines, count):
    total, width = lines.shape
    piece = width // CUT
    return call(
        unpack_kernel,
        "unpack",
        jax.ShapeDtypeStruct((count, CUT * width), BF16),
        grid=(CUT,),
        in_specs=[whole(either.shape), pl.BlockSpec((total, piece), lambda n: (0, n))],
        out_specs=whole((count, CUT * width)),
    )(either, lines)


def body(tokens, grad_out, router_logits, group_id, expert_ids, w_gate, w_up, w_down):
    count = tokens.shape[0]
    expert_total = lax.axis_size(NODE)
    sides = lax.axis_size("h")
    peers = expert_total * sides
    spread = jnp.asarray(order_matrix(sides))
    order = order_matrix(1)
    to_travel, in_order = jnp.asarray(order), jnp.asarray(order.T)

    tokens_out, slot = pack_tokens(group_id, expert_ids, tokens, spread, expert_total)

    inside = group_id < expert_total // GSIZE
    chosen = group_id[:, None] * GSIZE + expert_ids
    weights, pull_back = jax.vjp(
        lambda values: gate_weights(values, group_id, chosen, inside), router_logits
    )
    grads_out = pack_grads(slot, weights.T, grad_out, spread, expert_total)

    line = np.arange(peers * LINES)
    line_key = ((line // LINES // sides * CAP + line % CAP) * CUT + line // CAP % CUT)[None, :]
    chunk = jnp.arange(CUT, dtype=jnp.int32)[:, None]

    def lines_of(slots):
        key = jnp.where(slots[None] >= 0, slots[None] * CUT + chunk, -1).reshape(CUT * count, 1)
        return key == line_key.astype(np.int32)

    first, second = lines_of(slot[0]), lines_of(slot[1])
    either = (first | second).astype(BF16)
    first, second = first.astype(BF16), second.astype(BF16)

    tokens_in, grads_out, first, second, either = lax.optimization_barrier(
        (exchange(tokens_out), grads_out, first, second, either)
    )
    grads_in = exchange(grads_out)
    lines_other = swap(tokens_in)
    weights3 = (w_gate, w_up, w_down)
    rows_own, gate_own, up_own, hidden_own = forward(tokens_in, in_order, *weights3, True)
    lines_other, hidden_own = lax.optimization_barrier((lines_other, hidden_own))
    rows_other, gate_other, up_other, hidden_other, out_other = forward(
        lines_other, in_order, *weights3, False
    )
    out_lines = to_lines(product_out(hidden_own, w_down), swap(out_other), to_travel)
    out_lines, grads_in = lax.optimization_barrier((out_lines, grads_in))
    out_back = exchange(out_lines)

    lines_other = swap(grads_in)
    grads_own, dg_own, du_own = backward(
        grads_in, in_order, w_down, gate_own, up_own, w_gate, w_up, True
    )
    lines_other, dg_own, du_own = lax.optimization_barrier((lines_other, dg_own, du_own))
    grads_other, dg_other, du_other, in_other = backward(
        lines_other, in_order, w_down, gate_other, up_other, w_gate, w_up, False
    )
    in_lines = to_lines(product_in(dg_own, du_own, w_gate, w_up), swap(in_other), to_travel)
    in_lines, out_back, *halves = lax.optimization_barrier(
        (
            in_lines,
            out_back,
            (rows_own, rows_other),
            (grads_own, grads_other),
            jnp.concatenate([hidden_own, hidden_other]),
            jnp.concatenate([dg_own, dg_other]),
            jnp.concatenate([du_own, du_other]),
        )
    )
    in_back = exchange(in_lines)

    rows, grads = (jnp.concatenate(pair) for pair in halves[:2])
    hidden, dg, du = halves[2:]
    grad_gate = dot(rows, dg, ((0,), (0,))).astype(BF16)
    grad_up = dot(rows, du, ((0,), (0,))).astype(BF16)
    grad_down = dot(hidden, grads, ((0,), (0,))).astype(BF16)
    grad_down, out_back = lax.optimization_barrier((grad_down, out_back))
    mixed, scores = mix(first, second, out_back, grad_out, weights)
    d_logits = pull_back(scores)[0]
    d_tokens = unpack(either, in_back, count)
    return (mixed, d_tokens, d_logits, grad_gate[None], grad_up[None], grad_down[None])


def solution(mesh):
    fine = Mesh(mesh.devices.reshape(4, 4, 2, 2, 2), ALL)
    return jax.shard_map(
        body,
        mesh=fine,
        in_specs=(
            P(ALL, None),
            P(ALL, None),
            P(ALL, None),
            P(ALL),
            P(ALL, None),
            P(NODE, None, LOCAL),
            P(NODE, None, LOCAL),
            P(NODE, LOCAL, None),
        ),
        out_specs=(
            P(ALL, None),
            P(ALL, None),
            P(ALL, None),
            P(NODE, None, LOCAL),
            P(NODE, None, LOCAL),
            P(NODE, LOCAL, None),
        ),
        check_vma=False,
    )
```

```python
import functools

import jax
import jax.numpy as jnp
import numpy as np
from jax import lax
from jax.experimental import pallas as pl
from jax.experimental.pallas import tpu as pltpu
from jax.sharding import Mesh, PartitionSpec as P

GSIZE = 8
CAP = 6
CUT = 4
TEAM = 8
LINES = CUT * CAP
BUSY = 200_000_000_000
WIDE = ("y", "x", "l", "h")
ALL = ("y", "x", "l", "h", "c")
NODE = ("y", "x", "l")
LOCAL = ("h", "c")
F32 = jnp.float32
BF16 = jnp.bfloat16


def dot(a, b, dims=((1,), (0,))):
    return lax.dot_general(a, b, (dims, ((), ())), preferred_element_type=F32)


def across(a, b):
    return dot(a, b, ((1,), (1,)))


def call(kernel, name, outs, flops=1, **more):
    return pl.pallas_call(
        kernel,
        out_shape=outs,
        name=name,
        cost_estimate=pl.CostEstimate(flops=flops, bytes_accessed=1, transcendentals=0),
        compiler_params=pltpu.CompilerParams(vmem_limit_bytes=52 << 20),
        **more,
    )


def whole(shape):
    return pl.BlockSpec(shape, lambda *_: (0,) * len(shape))


def gate_weights(logits, group_ids, chosen, inside):
    probabilities = jax.nn.softmax(logits, axis=-1)
    columns = jnp.arange(logits.shape[1], dtype=jnp.int32)
    member = ((columns // GSIZE)[None, :] == group_ids[:, None]).astype(logits.dtype)
    group_mass = jnp.sum(probabilities * member, axis=1)
    picked = jnp.sum(
        jnp.where(chosen[:, :, None] == columns[None, None, :], logits[:, None, :], 0.0), axis=2
    )
    pair_share = jax.nn.softmax(picked, axis=-1)
    return jnp.where(inside[:, None], group_mass[:, None] * pair_share, 0.0)


def exchange(value):
    blocks = value.reshape(-1, LINES, value.shape[-1])
    out = lax.all_to_all(blocks, WIDE, split_axis=0, concat_axis=0, tiled=True)
    return out.reshape(value.shape)


def swap(value):
    return lax.ppermute(value, "c", [(0, 1), (1, 0)])


def order_matrix(copies):
    line = np.arange(TEAM * copies * LINES)
    member, chunk, slot = line // (copies * LINES), line // CAP % CUT, line % CAP
    wanted = (chunk * TEAM + member) * CAP + slot
    return (wanted[:, None] == np.arange(TEAM * LINES)[None, :]).astype(BF16)


def gathered(ref, start, width):
    team = pl.ds(start, TEAM * CAP)
    return jnp.concatenate([ref[team, j * width : (j + 1) * width] for j in range(CUT)], axis=0)


def spread_matrix(shape):
    copies = shape[0] // shape[1]
    line = lax.broadcasted_iota(jnp.int32, (shape[0], 1), 0)
    member, chunk, slot = line // (copies * LINES), line // CAP % CUT, line % CAP
    wanted = (chunk * TEAM + member) * CAP + slot
    return (wanted == lax.broadcasted_iota(jnp.int32, shape, 1)).astype(F32).astype(BF16)


def slots_kernel(expert_total, group_ref, expert_ref, rows_ref, out_ref, slot_ref, held, spread):
    team = pl.program_id(0)
    width = out_ref.shape[1]

    @pl.when(team == 0)
    def _():
        count = group_ref.shape[1]
        group = group_ref[...]
        inside = group < expert_total // GSIZE
        down = lax.broadcasted_iota(jnp.int32, (count, count), 0)
        along = lax.broadcasted_iota(jnp.int32, (count, count), 1)
        expert = lax.broadcasted_iota(jnp.int32, (expert_total, count), 0)
        targets, hots = [], []
        for k in range(2):
            column = expert_ref[:, k : k + 1].astype(F32)
            row = jnp.sum(jnp.where(down == along, column, 0.0), axis=0, keepdims=True)
            target = jnp.where(inside, group * GSIZE + row.astype(jnp.int32), expert_total)
            targets.append(target)
            hots.append((expert == target).astype(F32))
        before = (down < along).astype(F32).astype(BF16)
        earlier = dot((hots[0] + hots[1]).astype(BF16), before)
        place = lax.broadcasted_iota(jnp.int32, (expert_total * CAP, count), 0)
        picked = None
        for k in range(2):
            rank = jnp.sum(hots[k] * earlier, axis=0, keepdims=True).astype(jnp.int32)
            slot = jnp.where(inside, targets[k] * CAP + rank, -1)
            slot_ref[k : k + 1, :] = slot
            match = place == slot
            picked = match if picked is None else picked | match
        picked = picked.astype(F32).astype(BF16)
        held[...] = dot(picked, rows_ref[...]).astype(BF16)
        spread[...] = spread_matrix(spread.shape)

    start = pl.multiple_of(team * (TEAM * CAP), 16)
    out_ref[...] = dot(spread[...], gathered(held, start, width)).astype(BF16)


def pack_tokens(group_id, expert_ids, tokens, copies, expert_total):
    count, model_width = tokens.shape
    width = model_width // CUT
    teams, lines = expert_total // TEAM, TEAM * copies * LINES
    return call(
        functools.partial(slots_kernel, expert_total),
        "pack_tokens",
        (
            jax.ShapeDtypeStruct((teams * lines, width), BF16),
            jax.ShapeDtypeStruct((2, count), jnp.int32),
        ),
        grid=(teams,),
        in_specs=[
            whole((1, count)),
            whole(expert_ids.shape),
            whole(tokens.shape),
        ],
        out_specs=(pl.BlockSpec((lines, width), lambda t: (t, 0)), whole((2, count))),
        scratch_shapes=[
            pltpu.VMEM((expert_total * CAP, model_width), BF16),
            pltpu.VMEM((lines, TEAM * LINES), BF16),
        ],
    )(group_id[None], expert_ids, tokens)


def grads_kernel(slot_ref, weight_ref, rows_ref, spread_ref, out_ref, held):
    team = pl.program_id(0)
    width = out_ref.shape[1]

    @pl.when(team == 0)
    def _():
        place = lax.broadcasted_iota(jnp.int32, (held.shape[0], slot_ref.shape[1]), 0)
        first, second = place == slot_ref[0:1, :], place == slot_ref[1:2, :]
        weight = jnp.where(first, weight_ref[0:1, :], 0.0)
        weight += jnp.where(second, weight_ref[1:2, :], 0.0)
        weight = jnp.sum(weight, axis=1, keepdims=True)
        picked = (first | second).astype(F32).astype(BF16)
        held[...] = (dot(picked, rows_ref[...]) * weight).astype(BF16)

    start = pl.multiple_of(team * (TEAM * CAP), 16)
    out_ref[...] = dot(spread_ref[...], gathered(held, start, width)).astype(BF16)


def pack_grads(slot, weights, grad_out, spread, expert_total):
    count, model_width = grad_out.shape
    width = model_width // CUT
    teams, lines = expert_total // TEAM, spread.shape[0]
    return call(
        grads_kernel,
        "pack_grads",
        jax.ShapeDtypeStruct((teams * lines, width), BF16),
        grid=(teams,),
        in_specs=[
            whole((2, count)),
            whole((2, count)),
            whole(grad_out.shape),
            whole(spread.shape),
        ],
        out_specs=pl.BlockSpec((lines, width), lambda t: (t, 0)),
        scratch_shapes=[pltpu.VMEM((expert_total * CAP, model_width), BF16)],
    )(slot, weights, grad_out, spread)


def put_in_order(lines_ref, order_ref, rows_ref):
    width = lines_ref.shape[1]
    step, rows = TEAM * LINES, TEAM * CAP
    for t in range(lines_ref.shape[0] // step):
        moved = dot(order_ref[...], lines_ref[t * step : (t + 1) * step]).astype(BF16)
        for j in range(CUT):
            columns = slice(j * width, (j + 1) * width)
            rows_ref[t * rows : (t + 1) * rows, columns] = moved[j * rows : (j + 1) * rows]


def forward_kernel(
    lines_ref, order_ref, gate_ref, up_ref, down_ref, rows_ref, g_ref, u_ref, hidden_ref, *out_ref
):
    step = pl.program_id(0)
    width = lines_ref.shape[1]

    @pl.when(step == 0)
    def _():
        put_in_order(lines_ref, order_ref, rows_ref)
        g_ref[...] = jnp.zeros_like(g_ref)
        u_ref[...] = jnp.zeros_like(u_ref)

    rows = rows_ref[:, pl.ds(pl.multiple_of(step * width, width), width)]
    g_ref[...] += dot(rows, gate_ref[...])
    u_ref[...] += dot(rows, up_ref[...])

    @pl.when(step == pl.num_programs(0) - 1)
    def _():
        gate = g_ref[...]
        hidden = (gate * jax.nn.sigmoid(gate) * u_ref[...]).astype(BF16)
        hidden_ref[...] = hidden
        for ref in out_ref:
            for j in range(CUT):
                part = slice(j * width, (j + 1) * width)
                ref[:, part] = dot(hidden, down_ref[:, part]).astype(BF16)


def forward(lines, order, w_gate, w_up, w_down, own):
    width = lines.shape[1]
    half, model_width = lines.shape[0] // CUT, CUT * width
    units = w_down.shape[1]
    wide = jax.ShapeDtypeStruct((half, model_width), BF16)
    weight_spec = pl.BlockSpec((None, width, units), lambda k: (0, k, 0))
    act = whole((half, units))
    outs = [wide] + [jax.ShapeDtypeStruct((half, units), t) for t in (F32, F32, BF16)]
    if not own:
        outs.append(wide)
    down_shape = (None, units, model_width if not own else width)
    return call(
        forward_kernel,
        "forward_own" if own else "forward_other",
        outs,
        BUSY,
        grid=(CUT,),
        in_specs=[
            whole(lines.shape),
            whole(order.shape),
            weight_spec,
            weight_spec,
            pl.BlockSpec(down_shape, lambda k: (0, 0, 0)),
        ],
        out_specs=[whole(wide.shape), act, act, act, whole(wide.shape)][: len(outs)],
    )(lines, order, w_gate, w_up, w_down)


def backward_kernel(
    lines_ref, order_ref, down_ref, g_ref, u_ref, gate_ref, up_ref, rows_ref, dg_ref, du_ref, *more
):
    step = pl.program_id(0)
    width = lines_ref.shape[1]
    *out_ref, total = more

    @pl.when(step == 0)
    def _():
        put_in_order(lines_ref, order_ref, rows_ref)
        total[...] = jnp.zeros_like(total)

    rows = rows_ref[:, pl.ds(pl.multiple_of(step * width, width), width)]
    total[...] += across(rows, down_ref[...])

    @pl.when(step == pl.num_programs(0) - 1)
    def _():
        gate, grad_hidden = g_ref[...], total[...]
        sigmoid_gate = jax.nn.sigmoid(gate)
        dg = grad_hidden * u_ref[...] * sigmoid_gate * (1.0 + gate * (1.0 - sigmoid_gate))
        dg = dg.astype(BF16)
        du = (grad_hidden * (gate * sigmoid_gate)).astype(BF16)
        dg_ref[...] = dg
        du_ref[...] = du
        for ref in out_ref:
            for j in range(CUT):
                part = slice(j * width, (j + 1) * width)
                ref[:, part] = (
                    across(dg, gate_ref[part, :]) + across(du, up_ref[part, :])
                ).astype(BF16)


def backward(lines, order, w_down, gate_pre, up_pre, w_gate, w_up, own):
    width = lines.shape[1]
    half, model_width = lines.shape[0] // CUT, CUT * width
    units = w_down.shape[1]
    wide = jax.ShapeDtypeStruct((half, model_width), BF16)
    weight_shape = (None, model_width if not own else units, units)
    weight_spec = pl.BlockSpec(weight_shape, lambda k: (0, 0, 0))
    act = whole((half, units))
    outs = [wide] + [jax.ShapeDtypeStruct((half, units), BF16)] * 2
    if not own:
        outs.append(wide)
    return call(
        backward_kernel,
        "backward_own" if own else "backward_other",
        outs,
        BUSY,
        grid=(CUT,),
        in_specs=[
            whole(lines.shape),
            whole(order.shape),
            pl.BlockSpec((None, units, width), lambda k: (0, 0, k)),
            act,
            act,
            weight_spec,
            weight_spec,
        ],
        out_specs=[whole(wide.shape), act, act, whole(wide.shape)][: len(outs)],
        scratch_shapes=[pltpu.VMEM((half, units), F32)],
    )(lines, order, w_down, gate_pre, up_pre, w_gate, w_up)


def out_kernel(hidden_ref, down_ref, total_ref):
    total_ref[...] = dot(hidden_ref[...], down_ref[...])


def product_out(hidden, w_down):
    half, units = hidden.shape
    model_width = w_down.shape[2]
    width = model_width // CUT
    return call(
        out_kernel,
        "product_out",
        jax.ShapeDtypeStruct((half, model_width), F32),
        BUSY,
        grid=(CUT,),
        in_specs=[
            whole((half, units)),
            pl.BlockSpec((None, units, width), lambda k: (0, 0, k)),
        ],
        out_specs=pl.BlockSpec((half, width), lambda k: (0, k)),
    )(hidden, w_down)


def in_kernel(dg_ref, du_ref, gate_ref, up_ref, total_ref):
    total_ref[...] = across(dg_ref[...], gate_ref[...]) + across(du_ref[...], up_ref[...])


def product_in(dg, du, w_gate, w_up):
    half, units = dg.shape
    model_width = w_gate.shape[1]
    width = model_width // CUT
    weight_spec = pl.BlockSpec((None, width, units), lambda k: (0, k, 0))
    return call(
        in_kernel,
        "product_in",
        jax.ShapeDtypeStruct((half, model_width), F32),
        BUSY,
        grid=(CUT,),
        in_specs=[whole((half, units)), whole((half, units)), weight_spec, weight_spec],
        out_specs=pl.BlockSpec((half, width), lambda k: (0, k)),
    )(dg, du, w_gate, w_up)


def lines_kernel(total_ref, arrived_ref, order_ref, out_ref):
    width = out_ref.shape[1]
    rows, step = TEAM * CAP, TEAM * LINES
    for t in range(total_ref.shape[0] // rows):
        team = slice(t * rows, (t + 1) * rows)
        pieces = []
        for j in range(CUT):
            part = slice(j * width, (j + 1) * width)
            pieces.append((total_ref[team, part] + arrived_ref[team, part].astype(F32)).astype(BF16))
        held = jnp.concatenate(pieces, axis=0)
        out_ref[t * step : (t + 1) * step, :] = dot(order_ref[...], held).astype(BF16)


def to_lines(total, arrived, order):
    half, model_width = total.shape
    width = model_width // CUT
    parts = 4
    rows = half // parts
    return call(
        lines_kernel,
        "to_lines",
        jax.ShapeDtypeStruct((half * CUT, width), BF16),
        grid=(parts,),
        in_specs=[
            pl.BlockSpec((rows, model_width), lambda k: (k, 0)),
            pl.BlockSpec((rows, model_width), lambda k: (k, 0)),
            whole(order.shape),
        ],
        out_specs=pl.BlockSpec((rows * CUT, width), lambda k: (k, 0)),
    )(total, arrived, order)


def columns_grad_kernel(own, other, dg_own, dg_other, du_own, du_other, gate_ref, up_ref):
    rows_own, rows_other = own[...].T, other[...].T
    gate_ref[...] = (dot(rows_own, dg_own[...]) + dot(rows_other, dg_other[...])).astype(BF16)
    up_ref[...] = (dot(rows_own, du_own[...]) + dot(rows_other, du_other[...])).astype(BF16)


def columns_grad(rows, dg, du):
    half, model_width = rows[0].shape
    units = dg[0].shape[1]
    piece = model_width // 8
    rows_spec = pl.BlockSpec((half, piece), lambda k: (0, k))
    out_spec = pl.BlockSpec((None, piece, units), lambda k: (0, k, 0))
    return call(
        columns_grad_kernel,
        "columns_grad",
        [jax.ShapeDtypeStruct((1, model_width, units), BF16)] * 2,
        grid=(model_width // piece,),
        in_specs=[rows_spec] * 2 + [whole((half, units))] * 4,
        out_specs=[out_spec] * 2,
    )(*rows, *dg, *du)


def rows_grad_kernel(hidden_own, hidden_other, own, other, down_ref):
    down_ref[...] = (
        dot(hidden_own[...].T, own[...]) + dot(hidden_other[...].T, other[...])
    ).astype(BF16)


def rows_grad(hidden, grads):
    half, model_width = grads[0].shape
    units = hidden[0].shape[1]
    piece = model_width // CUT
    rows_spec = pl.BlockSpec((half, piece), lambda k: (0, k))
    return call(
        rows_grad_kernel,
        "rows_grad",
        jax.ShapeDtypeStruct((1, units, model_width), BF16),
        grid=(CUT,),
        in_specs=[whole((half, units))] * 2 + [rows_spec] * 2,
        out_specs=pl.BlockSpec((None, units, piece), lambda k: (0, 0, k)),
    )(*hidden, *grads)


def mix_kernel(first_ref, second_ref, lines_ref, grad_ref, weight_ref, mixed_ref, score_ref):
    step = pl.program_id(0)
    count, piece = grad_ref.shape[0], lines_ref.shape[1]
    width = grad_ref.shape[1] // CUT

    @pl.when(step == 0)
    def _():
        score_ref[...] = jnp.zeros_like(score_ref)

    first = dot(first_ref[...], lines_ref[...])
    second = dot(second_ref[...], lines_ref[...])
    for j in range(CUT):
        rows = slice(j * count, (j + 1) * count)
        columns = pl.ds(pl.multiple_of(j * width + step * piece, piece), piece)
        grad = grad_ref[:, columns].astype(F32)
        mixed_ref[:, columns] = (
            weight_ref[:, 0:1] * first[rows] + weight_ref[:, 1:2] * second[rows]
        ).astype(BF16)
        score_ref[:, 0:1] += jnp.sum(grad * first[rows], axis=1, keepdims=True)
        score_ref[:, 1:2] += jnp.sum(grad * second[rows], axis=1, keepdims=True)


def mix(first, second, lines, grad_out, weights):
    total, width = lines.shape
    piece = width // CUT
    return call(
        mix_kernel,
        "mix",
        (
            jax.ShapeDtypeStruct(grad_out.shape, BF16),
            jax.ShapeDtypeStruct(weights.shape, F32),
        ),
        grid=(CUT,),
        in_specs=[
            whole(first.shape),
            whole(second.shape),
            pl.BlockSpec((total, piece), lambda n: (0, n)),
            whole(grad_out.shape),
            whole(weights.shape),
        ],
        out_specs=(whole(grad_out.shape), whole(weights.shape)),
    )(first, second, lines, grad_out, weights)


def unpack_kernel(either_ref, lines_ref, out_ref):
    step = pl.program_id(0)
    count, piece = out_ref.shape[0], lines_ref.shape[1]
    width = out_ref.shape[1] // CUT
    rows = dot(either_ref[...], lines_ref[...]).astype(BF16)
    for j in range(CUT):
        columns = pl.ds(pl.multiple_of(j * width + step * piece, piece), piece)
        out_ref[:, columns] = rows[j * count : (j + 1) * count]


def unpack(either, lines, count):
    total, width = lines.shape
    piece = width // CUT
    return call(
        unpack_kernel,
        "unpack",
        jax.ShapeDtypeStruct((count, CUT * width), BF16),
        grid=(CUT,),
        in_specs=[whole(either.shape), pl.BlockSpec((total, piece), lambda n: (0, n))],
        out_specs=whole((count, CUT * width)),
    )(either, lines)


def body(tokens, grad_out, router_logits, group_id, expert_ids, w_gate, w_up, w_down):
    count = tokens.shape[0]
    expert_total = lax.axis_size(NODE)
    sides = lax.axis_size("h")
    peers = expert_total * sides
    spread = jnp.asarray(order_matrix(sides))
    order = order_matrix(1)
    to_travel, in_order = jnp.asarray(order), jnp.asarray(order.T)

    tokens_out, slot = pack_tokens(group_id, expert_ids, tokens, sides, expert_total)

    inside = group_id < expert_total // GSIZE
    chosen = group_id[:, None] * GSIZE + expert_ids
    weights, pull_back = jax.vjp(
        lambda values: gate_weights(values, group_id, chosen, inside), router_logits
    )
    grads_out = pack_grads(slot, weights.T, grad_out, spread, expert_total)

    line = np.arange(peers * LINES)
    line_key = ((line // LINES // sides * CAP + line % CAP) * CUT + line // CAP % CUT)[None, :]
    chunk = jnp.arange(CUT, dtype=jnp.int32)[:, None]

    def lines_of(slots):
        key = jnp.where(slots[None] >= 0, slots[None] * CUT + chunk, -1).reshape(CUT * count, 1)
        return key == line_key.astype(np.int32)

    first, second = lines_of(slot[0]), lines_of(slot[1])
    either = (first | second).astype(BF16)
    first, second = first.astype(BF16), second.astype(BF16)

    tokens_in, grads_out, first, second, either = lax.optimization_barrier(
        (exchange(tokens_out), grads_out, first, second, either)
    )
    grads_in = exchange(grads_out)
    lines_other = swap(tokens_in)
    weights3 = (w_gate, w_up, w_down)
    rows_own, gate_own, up_own, hidden_own = forward(tokens_in, in_order, *weights3, True)
    lines_other, hidden_own = lax.optimization_barrier((lines_other, hidden_own))
    rows_other, gate_other, up_other, hidden_other, out_other = forward(
        lines_other, in_order, *weights3, False
    )
    out_lines = to_lines(product_out(hidden_own, w_down), swap(out_other), to_travel)
    out_lines, grads_in = lax.optimization_barrier((out_lines, grads_in))
    out_back = exchange(out_lines)

    lines_other = swap(grads_in)
    grads_own, dg_own, du_own = backward(
        grads_in, in_order, w_down, gate_own, up_own, w_gate, w_up, True
    )
    lines_other, dg_own, du_own = lax.optimization_barrier((lines_other, dg_own, du_own))
    grads_other, dg_other, du_other, in_other = backward(
        lines_other, in_order, w_down, gate_other, up_other, w_gate, w_up, False
    )
    in_lines = to_lines(product_in(dg_own, du_own, w_gate, w_up), swap(in_other), to_travel)
    in_lines, out_back, rows, grads, hidden, dg, du = lax.optimization_barrier(
        (
            in_lines,
            out_back,
            (rows_own, rows_other),
            (grads_own, grads_other),
            (hidden_own, hidden_other),
            (dg_own, dg_other),
            (du_own, du_other),
        )
    )
    in_back = exchange(in_lines)

    grad_gate, grad_up = columns_grad(rows, dg, du)
    grad_down = rows_grad(hidden, grads)
    mixed, scores = mix(first, second, out_back, grad_out, weights)
    d_logits = pull_back(scores)[0]
    d_tokens = unpack(either, in_back, count)
    return (mixed, d_tokens, d_logits, grad_gate, grad_up, grad_down)


def solution(mesh):
    fine = Mesh(mesh.devices.reshape(4, 4, 2, 2, 2), ALL)
    return jax.shard_map(
        body,
        mesh=fine,
        in_specs=(
            P(ALL, None),
            P(ALL, None),
            P(ALL, None),
            P(ALL),
            P(ALL, None),
            P(NODE, None, LOCAL),
            P(NODE, None, LOCAL),
            P(NODE, LOCAL, None),
        ),
        out_specs=(
            P(ALL, None),
            P(ALL, None),
            P(ALL, None),
            P(NODE, None, LOCAL),
            P(NODE, None, LOCAL),
            P(NODE, LOCAL, None),
        ),
        check_vma=False,
    )
```

```python
import functools

import jax
import jax.numpy as jnp
import numpy as np
from jax import lax
from jax.experimental import pallas as pl
from jax.experimental.pallas import tpu as pltpu
from jax.sharding import Mesh, PartitionSpec as P

GSIZE = 8
CAP = 6
CUT = 4
TEAM = 8
LINES = CUT * CAP
BUSY = 200_000_000_000
WIDE = ("h", "y", "x", "l")
ALL = ("y", "x", "l", "h", "c")
NODE = ("y", "x", "l")
LOCAL = ("h", "c")
F32 = jnp.float32
BF16 = jnp.bfloat16


def dot(a, b, dims=((1,), (0,))):
    return lax.dot_general(a, b, (dims, ((), ())), preferred_element_type=F32)


def across(a, b):
    return dot(a, b, ((1,), (1,)))


def call(kernel, name, outs, flops=1, **more):
    return pl.pallas_call(
        kernel,
        out_shape=outs,
        name=name,
        cost_estimate=pl.CostEstimate(flops=flops, bytes_accessed=1, transcendentals=0),
        compiler_params=pltpu.CompilerParams(vmem_limit_bytes=52 << 20),
        **more,
    )


def in_hbm(value):
    return pltpu.with_memory_space_constraint(value, pltpu.HBM)


def whole(shape):
    return pl.BlockSpec(shape, lambda *_: (0,) * len(shape))


def gate_weights(logits, group_ids, chosen, inside):
    probabilities = jax.nn.softmax(logits, axis=-1)
    columns = jnp.arange(logits.shape[1], dtype=jnp.int32)
    member = ((columns // GSIZE)[None, :] == group_ids[:, None]).astype(logits.dtype)
    group_mass = jnp.sum(probabilities * member, axis=1)
    picked = jnp.sum(
        jnp.where(chosen[:, :, None] == columns[None, None, :], logits[:, None, :], 0.0), axis=2
    )
    pair_share = jax.nn.softmax(picked, axis=-1)
    return jnp.where(inside[:, None], group_mass[:, None] * pair_share, 0.0)


def exchange(value):
    blocks = value.reshape(-1, LINES, value.shape[-1])
    out = lax.all_to_all(blocks, WIDE, split_axis=0, concat_axis=0, tiled=True)
    return out.reshape(-1, value.shape[-1])


def swap(value):
    return lax.ppermute(value, "c", [(0, 1), (1, 0)])


def order_matrix():
    line = np.arange(TEAM * LINES)
    member, chunk, slot = line // LINES, line // CAP % CUT, line % CAP
    wanted = (chunk * TEAM + member) * CAP + slot
    return (wanted[:, None] == line[None, :]).astype(BF16)


def gathered(ref, start, width):
    team = pl.ds(start, TEAM * CAP)
    return jnp.concatenate([ref[team, j * width : (j + 1) * width] for j in range(CUT)], axis=0)


def order_in_kernel(shape):
    line = lax.broadcasted_iota(jnp.int32, (shape[0], 1), 0)
    member, chunk, slot = line // LINES, line // CAP % CUT, line % CAP
    wanted = (chunk * TEAM + member) * CAP + slot
    return (wanted == lax.broadcasted_iota(jnp.int32, shape, 1)).astype(F32).astype(BF16)


def send_team(held, order, out_ref):
    team, width = pl.program_id(0), out_ref.shape[2]
    start = pl.multiple_of(team * (TEAM * CAP), 16)
    lines = dot(order, gathered(held, start, width)).astype(BF16)
    for side in range(out_ref.shape[0]):
        out_ref[side] = lines


def slots_kernel(expert_total, group_in, expert_in, rows_in, out_ref, slot_ref, held, order, *own):
    group_ref, expert_ref, rows_ref, sems = own

    @pl.when(pl.program_id(0) == 0)
    def _():
        pairs = ((group_in, group_ref), (expert_in, expert_ref), (rows_in, rows_ref))
        copies = [
            pltpu.make_async_copy(src, dst, sems.at[k]) for k, (src, dst) in enumerate(pairs)
        ]
        for copy in copies:
            copy.start()
        order[...] = order_in_kernel(order.shape)
        copies[0].wait()
        copies[1].wait()
        count = group_ref.shape[1]
        group = group_ref[...]
        inside = group < expert_total // GSIZE
        down = lax.broadcasted_iota(jnp.int32, (count, count), 0)
        along = lax.broadcasted_iota(jnp.int32, (count, count), 1)
        expert = lax.broadcasted_iota(jnp.int32, (expert_total, count), 0)
        targets, hots = [], []
        for k in range(2):
            target = jnp.where(inside, group * GSIZE + expert_ref[k : k + 1, :], expert_total)
            targets.append(target)
            hots.append((expert == target).astype(F32))
        before = (down < along).astype(F32).astype(BF16)
        earlier = dot((hots[0] + hots[1]).astype(BF16), before)
        place = lax.broadcasted_iota(jnp.int32, (expert_total * CAP, count), 0)
        picked = None
        for k in range(2):
            rank = jnp.sum(hots[k] * earlier, axis=0, keepdims=True).astype(jnp.int32)
            slot = jnp.where(inside, targets[k] * CAP + rank, -1)
            slot_ref[k : k + 1, :] = slot
            match = place == slot
            picked = match if picked is None else picked | match
        picked = picked.astype(F32).astype(BF16)
        copies[2].wait()
        held[...] = dot(picked, rows_ref[...]).astype(BF16)

    send_team(held, order[...], out_ref)


def lines_out(sides, teams, width):
    shape = jax.ShapeDtypeStruct((sides, teams * TEAM * LINES, width), BF16)
    return shape, pl.BlockSpec((sides, TEAM * LINES, width), lambda t: (0, t, 0))


def pack_tokens(group_id, expert_ids, tokens, sides, expert_total):
    count, model_width = tokens.shape
    teams = expert_total // TEAM
    shape, spec = lines_out(sides, teams, model_width // CUT)
    return call(
        functools.partial(slots_kernel, expert_total),
        "pack_tokens",
        (shape, jax.ShapeDtypeStruct((2, count), jnp.int32)),
        grid=(teams,),
        in_specs=[pl.BlockSpec(memory_space=pltpu.HBM)] * 3,
        out_specs=(spec, whole((2, count))),
        scratch_shapes=[
            pltpu.VMEM((expert_total * CAP, model_width), BF16),
            pltpu.VMEM((TEAM * LINES, TEAM * LINES), BF16),
            pltpu.VMEM((1, count), jnp.int32),
            pltpu.VMEM((2, count), jnp.int32),
            pltpu.VMEM((count, model_width), BF16),
            pltpu.SemaphoreType.DMA((3,)),
        ],
    )(*(in_hbm(value) for value in (group_id[None], expert_ids.T, tokens)))


def grads_kernel(slot_ref, weight_ref, rows_ref, order_ref, out_ref, held):
    @pl.when(pl.program_id(0) == 0)
    def _():
        place = lax.broadcasted_iota(jnp.int32, (held.shape[0], slot_ref.shape[1]), 0)
        first, second = place == slot_ref[0:1, :], place == slot_ref[1:2, :]
        weight = jnp.where(first, weight_ref[0:1, :], 0.0)
        weight += jnp.where(second, weight_ref[1:2, :], 0.0)
        weight = jnp.sum(weight, axis=1, keepdims=True)
        picked = (first | second).astype(F32).astype(BF16)
        held[...] = (dot(picked, rows_ref[...]) * weight).astype(BF16)

    send_team(held, order_ref[...], out_ref)


def pack_grads(slot, weights, grad_out, order, sides, expert_total):
    count, model_width = grad_out.shape
    teams = expert_total // TEAM
    shape, spec = lines_out(sides, teams, model_width // CUT)
    return call(
        grads_kernel,
        "pack_grads",
        shape,
        grid=(teams,),
        in_specs=[
            whole((2, count)),
            whole((2, count)),
            whole(grad_out.shape),
            whole(order.shape),
        ],
        out_specs=spec,
        scratch_shapes=[pltpu.VMEM((expert_total * CAP, model_width), BF16)],
    )(slot, weights, grad_out, order)


def put_in_order(lines_ref, order_ref, rows_ref):
    width = lines_ref.shape[1]
    step, rows = TEAM * LINES, TEAM * CAP
    for t in range(lines_ref.shape[0] // step):
        moved = dot(order_ref[...], lines_ref[t * step : (t + 1) * step]).astype(BF16)
        for j in range(CUT):
            columns = slice(j * width, (j + 1) * width)
            rows_ref[t * rows : (t + 1) * rows, columns] = moved[j * rows : (j + 1) * rows]


def forward_kernel(
    lines_ref, order_ref, gate_ref, up_ref, down_ref, rows_ref, g_ref, u_ref, hidden_ref, *out_ref
):
    step = pl.program_id(0)
    width = lines_ref.shape[1]

    @pl.when(step == 0)
    def _():
        put_in_order(lines_ref, order_ref, rows_ref)
        g_ref[...] = jnp.zeros_like(g_ref)
        u_ref[...] = jnp.zeros_like(u_ref)

    rows = rows_ref[:, pl.ds(pl.multiple_of(step * width, width), width)]
    g_ref[...] += dot(rows, gate_ref[...])
    u_ref[...] += dot(rows, up_ref[...])

    @pl.when(step == pl.num_programs(0) - 1)
    def _():
        gate = g_ref[...]
        hidden = (gate * jax.nn.sigmoid(gate) * u_ref[...]).astype(BF16)
        hidden_ref[...] = hidden
        for ref in out_ref:
            for j in range(CUT):
                part = slice(j * width, (j + 1) * width)
                ref[:, part] = dot(hidden, down_ref[:, part]).astype(BF16)


def forward(lines, order, w_gate, w_up, w_down, own):
    width = lines.shape[1]
    half, model_width = lines.shape[0] // CUT, CUT * width
    units = w_down.shape[1]
    wide = jax.ShapeDtypeStruct((half, model_width), BF16)
    weight_spec = pl.BlockSpec((None, width, units), lambda k: (0, k, 0))
    act = whole((half, units))
    outs = [wide] + [jax.ShapeDtypeStruct((half, units), t) for t in (F32, F32, BF16)]
    if not own:
        outs.append(wide)
    down_shape = (None, units, model_width if not own else width)
    return call(
        forward_kernel,
        "forward_own" if own else "forward_other",
        outs,
        BUSY,
        grid=(CUT,),
        in_specs=[
            whole(lines.shape),
            whole(order.shape),
            weight_spec,
            weight_spec,
            pl.BlockSpec(down_shape, lambda k: (0, 0, 0)),
        ],
        out_specs=[whole(wide.shape), act, act, act, whole(wide.shape)][: len(outs)],
    )(lines, order, w_gate, w_up, w_down)


def backward_kernel(
    lines_ref, order_ref, down_ref, g_ref, u_ref, gate_ref, up_ref, rows_ref, dg_ref, du_ref, *more
):
    step = pl.program_id(0)
    width = lines_ref.shape[1]
    *out_ref, total = more

    @pl.when(step == 0)
    def _():
        put_in_order(lines_ref, order_ref, rows_ref)
        total[...] = jnp.zeros_like(total)

    rows = rows_ref[:, pl.ds(pl.multiple_of(step * width, width), width)]
    total[...] += across(rows, down_ref[...])

    @pl.when(step == pl.num_programs(0) - 1)
    def _():
        gate, grad_hidden = g_ref[...], total[...]
        sigmoid_gate = jax.nn.sigmoid(gate)
        dg = grad_hidden * u_ref[...] * sigmoid_gate * (1.0 + gate * (1.0 - sigmoid_gate))
        dg = dg.astype(BF16)
        du = (grad_hidden * (gate * sigmoid_gate)).astype(BF16)
        dg_ref[...] = dg
        du_ref[...] = du
        for ref in out_ref:
            for j in range(CUT):
                part = slice(j * width, (j + 1) * width)
                ref[:, part] = (
                    across(dg, gate_ref[part, :]) + across(du, up_ref[part, :])
                ).astype(BF16)


def backward(lines, order, w_down, gate_pre, up_pre, w_gate, w_up, own):
    width = lines.shape[1]
    half, model_width = lines.shape[0] // CUT, CUT * width
    units = w_down.shape[1]
    wide = jax.ShapeDtypeStruct((half, model_width), BF16)
    weight_shape = (None, model_width if not own else units, units)
    weight_spec = pl.BlockSpec(weight_shape, lambda k: (0, 0, 0))
    act = whole((half, units))
    outs = [wide] + [jax.ShapeDtypeStruct((half, units), BF16)] * 2
    if not own:
        outs.append(wide)
    return call(
        backward_kernel,
        "backward_own" if own else "backward_other",
        outs,
        BUSY,
        grid=(CUT,),
        in_specs=[
            whole(lines.shape),
            whole(order.shape),
            pl.BlockSpec((None, units, width), lambda k: (0, 0, k)),
            act,
            act,
            weight_spec,
            weight_spec,
        ],
        out_specs=[whole(wide.shape), act, act, whole(wide.shape)][: len(outs)],
        scratch_shapes=[pltpu.VMEM((half, units), F32)],
    )(lines, order, w_down, gate_pre, up_pre, w_gate, w_up)


def out_kernel(hidden_ref, down_ref, total_ref):
    total_ref[...] = dot(hidden_ref[...], down_ref[...])


def product_out(hidden, w_down):
    half, units = hidden.shape
    model_width = w_down.shape[2]
    width = model_width // CUT
    return call(
        out_kernel,
        "product_out",
        jax.ShapeDtypeStruct((half, model_width), F32),
        BUSY,
        grid=(CUT,),
        in_specs=[
            whole((half, units)),
            pl.BlockSpec((None, units, width), lambda k: (0, 0, k)),
        ],
        out_specs=pl.BlockSpec((half, width), lambda k: (0, k)),
    )(hidden, w_down)


def in_kernel(dg_ref, du_ref, gate_ref, up_ref, total_ref):
    total_ref[...] = across(dg_ref[...], gate_ref[...]) + across(du_ref[...], up_ref[...])


def product_in(dg, du, w_gate, w_up):
    half, units = dg.shape
    model_width = w_gate.shape[1]
    width = model_width // CUT
    weight_spec = pl.BlockSpec((None, width, units), lambda k: (0, k, 0))
    return call(
        in_kernel,
        "product_in",
        jax.ShapeDtypeStruct((half, model_width), F32),
        BUSY,
        grid=(CUT,),
        in_specs=[whole((half, units)), whole((half, units)), weight_spec, weight_spec],
        out_specs=pl.BlockSpec((half, width), lambda k: (0, k)),
    )(dg, du, w_gate, w_up)


def lines_kernel(total_ref, arrived_ref, order_ref, out_ref):
    width = out_ref.shape[1]
    rows, step = TEAM * CAP, TEAM * LINES
    for t in range(total_ref.shape[0] // rows):
        team = slice(t * rows, (t + 1) * rows)
        pieces = []
        for j in range(CUT):
            part = slice(j * width, (j + 1) * width)
            pieces.append((total_ref[team, part] + arrived_ref[team, part].astype(F32)).astype(BF16))
        held = jnp.concatenate(pieces, axis=0)
        out_ref[t * step : (t + 1) * step, :] = dot(order_ref[...], held).astype(BF16)


def to_lines(total, arrived, order):
    half, model_width = total.shape
    width = model_width // CUT
    parts = 4
    rows = half // parts
    return call(
        lines_kernel,
        "to_lines",
        jax.ShapeDtypeStruct((half * CUT, width), BF16),
        grid=(parts,),
        in_specs=[
            pl.BlockSpec((rows, model_width), lambda k: (k, 0)),
            pl.BlockSpec((rows, model_width), lambda k: (k, 0)),
            whole(order.shape),
        ],
        out_specs=pl.BlockSpec((rows * CUT, width), lambda k: (k, 0)),
    )(total, arrived, order)


def columns_grad_kernel(own, other, dg_own, dg_other, du_own, du_other, gate_ref, up_ref):
    rows_own, rows_other = own[...].T, other[...].T
    gate_ref[...] = (dot(rows_own, dg_own[...]) + dot(rows_other, dg_other[...])).astype(BF16)
    up_ref[...] = (dot(rows_own, du_own[...]) + dot(rows_other, du_other[...])).astype(BF16)


def columns_grad(rows, dg, du):
    half, model_width = rows[0].shape
    units = dg[0].shape[1]
    piece = model_width // 8
    rows_spec = pl.BlockSpec((half, piece), lambda k: (0, k))
    out_spec = pl.BlockSpec((None, piece, units), lambda k: (0, k, 0))
    return call(
        columns_grad_kernel,
        "columns_grad",
        [jax.ShapeDtypeStruct((1, model_width, units), BF16)] * 2,
        grid=(model_width // piece,),
        in_specs=[rows_spec] * 2 + [whole((half, units))] * 4,
        out_specs=[out_spec] * 2,
    )(*rows, *dg, *du)


def rows_grad_kernel(hidden_own, hidden_other, own, other, down_ref):
    down_ref[...] = (
        dot(hidden_own[...].T, own[...]) + dot(hidden_other[...].T, other[...])
    ).astype(BF16)


def rows_grad(hidden, grads):
    half, model_width = grads[0].shape
    units = hidden[0].shape[1]
    piece = model_width // CUT
    rows_spec = pl.BlockSpec((half, piece), lambda k: (0, k))
    return call(
        rows_grad_kernel,
        "rows_grad",
        jax.ShapeDtypeStruct((1, units, model_width), BF16),
        grid=(CUT,),
        in_specs=[whole((half, units))] * 2 + [rows_spec] * 2,
        out_specs=pl.BlockSpec((None, units, piece), lambda k: (0, 0, k)),
    )(*hidden, *grads)


def both_chips(lines_ref):
    half = lines_ref.shape[0] // 2
    return (lines_ref[:half].astype(F32) + lines_ref[half:].astype(F32)).astype(BF16)


def mix_kernel(first_ref, second_ref, lines_ref, grad_ref, weight_ref, mixed_ref, score_ref):
    step = pl.program_id(0)
    count, piece = grad_ref.shape[0], lines_ref.shape[1]
    width = grad_ref.shape[1] // CUT

    @pl.when(step == 0)
    def _():
        score_ref[...] = jnp.zeros_like(score_ref)

    lines = both_chips(lines_ref)
    first = dot(first_ref[...], lines)
    second = dot(second_ref[...], lines)
    for j in range(CUT):
        rows = slice(j * count, (j + 1) * count)
        columns = pl.ds(pl.multiple_of(j * width + step * piece, piece), piece)
        grad = grad_ref[:, columns].astype(F32)
        mixed_ref[:, columns] = (
            weight_ref[:, 0:1] * first[rows] + weight_ref[:, 1:2] * second[rows]
        ).astype(BF16)
        score_ref[:, 0:1] += jnp.sum(grad * first[rows], axis=1, keepdims=True)
        score_ref[:, 1:2] += jnp.sum(grad * second[rows], axis=1, keepdims=True)


def mix(first, second, lines, grad_out, weights):
    total, width = lines.shape
    piece = width // CUT
    return call(
        mix_kernel,
        "mix",
        (
            jax.ShapeDtypeStruct(grad_out.shape, BF16),
            jax.ShapeDtypeStruct(weights.shape, F32),
        ),
        grid=(CUT,),
        in_specs=[
            whole(first.shape),
            whole(second.shape),
            pl.BlockSpec((total, piece), lambda n: (0, n)),
            whole(grad_out.shape),
            whole(weights.shape),
        ],
        out_specs=(whole(grad_out.shape), whole(weights.shape)),
    )(first, second, lines, grad_out, weights)


def unpack_kernel(either_ref, lines_ref, out_ref):
    step = pl.program_id(0)
    count, piece = out_ref.shape[0], lines_ref.shape[1]
    width = out_ref.shape[1] // CUT
    rows = dot(either_ref[...], both_chips(lines_ref)).astype(BF16)
    for j in range(CUT):
        columns = pl.ds(pl.multiple_of(j * width + step * piece, piece), piece)
        out_ref[:, columns] = rows[j * count : (j + 1) * count]


def unpack(either, lines, count):
    total, width = lines.shape
    piece = width // CUT
    return call(
        unpack_kernel,
        "unpack",
        jax.ShapeDtypeStruct((count, CUT * width), BF16),
        grid=(CUT,),
        in_specs=[whole(either.shape), pl.BlockSpec((total, piece), lambda n: (0, n))],
        out_specs=whole((count, CUT * width)),
    )(either, lines)


def body(tokens, grad_out, router_logits, group_id, expert_ids, w_gate, w_up, w_down):
    count = tokens.shape[0]
    expert_total = lax.axis_size(NODE)
    sides = lax.axis_size("h")
    order = order_matrix()
    to_travel, in_order = jnp.asarray(order), jnp.asarray(order.T)

    tokens_out, slot = pack_tokens(group_id, expert_ids, tokens, sides, expert_total)

    inside = group_id < expert_total // GSIZE
    chosen = group_id[:, None] * GSIZE + expert_ids
    weights, pull_back = jax.vjp(
        lambda values: gate_weights(values, group_id, chosen, inside), router_logits
    )
    grads_out = pack_grads(slot, weights.T, grad_out, to_travel, sides, expert_total)

    line = np.arange(expert_total * LINES)
    line_key = ((line // LINES * CAP + line % CAP) * CUT + line // CAP % CUT)[None, :]
    chunk = jnp.arange(CUT, dtype=jnp.int32)[:, None]

    def lines_of(slots):
        key = jnp.where(slots[None] >= 0, slots[None] * CUT + chunk, -1).reshape(CUT * count, 1)
        return key == line_key.astype(np.int32)

    first, second = lines_of(slot[0]), lines_of(slot[1])
    either = (first | second).astype(BF16)
    first, second = first.astype(BF16), second.astype(BF16)

    tokens_in, grads_out, first, second, either = lax.optimization_barrier(
        (exchange(tokens_out), grads_out, first, second, either)
    )
    grads_in = exchange(grads_out)
    lines_other = swap(tokens_in)
    weights3 = (w_gate, w_up, w_down)
    rows_own, gate_own, up_own, hidden_own = forward(tokens_in, in_order, *weights3, True)
    lines_other, hidden_own = lax.optimization_barrier((lines_other, hidden_own))
    rows_other, gate_other, up_other, hidden_other, out_other = forward(
        lines_other, in_order, *weights3, False
    )
    out_lines = to_lines(product_out(hidden_own, w_down), swap(out_other), to_travel)
    out_lines, grads_in = lax.optimization_barrier((out_lines, grads_in))
    out_back = exchange(out_lines)

    lines_other = swap(grads_in)
    grads_own, dg_own, du_own = backward(
        grads_in, in_order, w_down, gate_own, up_own, w_gate, w_up, True
    )
    lines_other, dg_own, du_own = lax.optimization_barrier((lines_other, dg_own, du_own))
    grads_other, dg_other, du_other, in_other = backward(
        lines_other, in_order, w_down, gate_other, up_other, w_gate, w_up, False
    )
    in_lines = to_lines(product_in(dg_own, du_own, w_gate, w_up), swap(in_other), to_travel)
    in_lines, out_back, rows, grads, hidden, dg, du = lax.optimization_barrier(
        (
            in_lines,
            out_back,
            (rows_own, rows_other),
            (grads_own, grads_other),
            (hidden_own, hidden_other),
            (dg_own, dg_other),
            (du_own, du_other),
        )
    )
    in_back = exchange(in_lines)

    grad_gate, grad_up = columns_grad(rows, dg, du)
    grad_down = rows_grad(hidden, grads)
    mixed, scores = mix(first, second, out_back, grad_out, weights)
    d_logits = pull_back(scores)[0]
    d_tokens = unpack(either, in_back, count)
    return (mixed, d_tokens, d_logits, grad_gate, grad_up, grad_down)


def solution(mesh):
    fine = Mesh(mesh.devices.reshape(4, 4, 2, 2, 2), ALL)
    return jax.shard_map(
        body,
        mesh=fine,
        in_specs=(
            P(ALL, None),
            P(ALL, None),
            P(ALL, None),
            P(ALL),
            P(ALL, None),
            P(NODE, None, LOCAL),
            P(NODE, None, LOCAL),
            P(NODE, LOCAL, None),
        ),
        out_specs=(
            P(ALL, None),
            P(ALL, None),
            P(ALL, None),
            P(NODE, None, LOCAL),
            P(NODE, None, LOCAL),
            P(NODE, LOCAL, None),
        ),
        check_vma=False,
    )
```

```python
import functools

import jax
import jax.numpy as jnp
import numpy as np
from jax import lax
from jax.experimental import pallas as pl
from jax.experimental.pallas import tpu as pltpu
from jax.sharding import Mesh, PartitionSpec as P

GSIZE = 8
CAP = 6
CUT = 4
TEAM = 8
LINES = CUT * CAP
BUSY = 200_000_000_000
WIDE = ("h", "y", "x", "l")
ALL = ("y", "x", "l", "h", "c")
NODE = ("y", "x", "l")
LOCAL = ("h", "c")
F32 = jnp.float32
BF16 = jnp.bfloat16


def dot(a, b, dims=((1,), (0,))):
    return lax.dot_general(a, b, (dims, ((), ())), preferred_element_type=F32)


def across(a, b):
    return dot(a, b, ((1,), (1,)))


def call(kernel, name, outs, flops=1, **more):
    return pl.pallas_call(
        kernel,
        out_shape=outs,
        name=name,
        cost_estimate=pl.CostEstimate(flops=flops, bytes_accessed=1, transcendentals=0),
        compiler_params=pltpu.CompilerParams(vmem_limit_bytes=52 << 20),
        **more,
    )


def in_hbm(value):
    return pltpu.with_memory_space_constraint(value, pltpu.HBM)


def whole(shape):
    return pl.BlockSpec(shape, lambda *_: (0,) * len(shape))


def gate_weights(logits, group_ids, chosen, inside):
    probabilities = jax.nn.softmax(logits, axis=-1)
    columns = jnp.arange(logits.shape[1], dtype=jnp.int32)
    member = ((columns // GSIZE)[None, :] == group_ids[:, None]).astype(logits.dtype)
    group_mass = jnp.sum(probabilities * member, axis=1)
    picked = jnp.sum(
        jnp.where(chosen[:, :, None] == columns[None, None, :], logits[:, None, :], 0.0), axis=2
    )
    pair_share = jax.nn.softmax(picked, axis=-1)
    return jnp.where(inside[:, None], group_mass[:, None] * pair_share, 0.0)


def exchange(value):
    blocks = value.reshape(-1, LINES, value.shape[-1])
    out = lax.all_to_all(blocks, WIDE, split_axis=0, concat_axis=0, tiled=True)
    return out.reshape(-1, value.shape[-1])


def swap(value):
    return lax.ppermute(value, "c", [(0, 1), (1, 0)])


def order_matrix():
    line = np.arange(TEAM * LINES)
    member, chunk, slot = line // LINES, line // CAP % CUT, line % CAP
    wanted = (chunk * TEAM + member) * CAP + slot
    return (wanted[:, None] == line[None, :]).astype(BF16)


def gathered(ref, start, width):
    team = pl.ds(start, TEAM * CAP)
    return jnp.concatenate([ref[team, j * width : (j + 1) * width] for j in range(CUT)], axis=0)


def order_in_kernel(shape):
    line = lax.broadcasted_iota(jnp.int32, (shape[0], 1), 0)
    member, chunk, slot = line // LINES, line // CAP % CUT, line % CAP
    wanted = (chunk * TEAM + member) * CAP + slot
    return (wanted == lax.broadcasted_iota(jnp.int32, shape, 1)).astype(F32).astype(BF16)


def send_team(held, order, out_ref):
    team, width = pl.program_id(0), out_ref.shape[2]
    start = pl.multiple_of(team * (TEAM * CAP), 16)
    lines = dot(order, gathered(held, start, width)).astype(BF16)
    for side in range(out_ref.shape[0]):
        out_ref[side] = lines


def slots_kernel(expert_total, group_in, expert_in, rows_in, out_ref, slot_ref, held, order, *own):
    group_ref, expert_ref, rows_ref, sems = own

    @pl.when(pl.program_id(0) == 0)
    def _():
        pairs = ((group_in, group_ref), (expert_in, expert_ref), (rows_in, rows_ref))
        copies = [
            pltpu.make_async_copy(src, dst, sems.at[k]) for k, (src, dst) in enumerate(pairs)
        ]
        for copy in copies:
            copy.start()
        order[...] = order_in_kernel(order.shape)
        copies[0].wait()
        copies[1].wait()
        count = group_ref.shape[1]
        group = group_ref[...]
        inside = group < expert_total // GSIZE
        down = lax.broadcasted_iota(jnp.int32, (count, count), 0)
        along = lax.broadcasted_iota(jnp.int32, (count, count), 1)
        expert = lax.broadcasted_iota(jnp.int32, (expert_total, count), 0)
        targets, hots = [], []
        for k in range(2):
            target = jnp.where(inside, group * GSIZE + expert_ref[k : k + 1, :], expert_total)
            targets.append(target)
            hots.append((expert == target).astype(F32))
        before = (down < along).astype(F32).astype(BF16)
        earlier = dot((hots[0] + hots[1]).astype(BF16), before)
        place = lax.broadcasted_iota(jnp.int32, (expert_total * CAP, count), 0)
        picked = None
        for k in range(2):
            rank = jnp.sum(hots[k] * earlier, axis=0, keepdims=True).astype(jnp.int32)
            slot = jnp.where(inside, targets[k] * CAP + rank, -1)
            slot_ref[k : k + 1, :] = slot
            match = place == slot
            picked = match if picked is None else picked | match
        picked = picked.astype(F32).astype(BF16)
        copies[2].wait()
        held[...] = dot(picked, rows_ref[...]).astype(BF16)

    send_team(held, order[...], out_ref)


def lines_out(sides, teams, width):
    shape = jax.ShapeDtypeStruct((sides, teams * TEAM * LINES, width), BF16)
    return shape, pl.BlockSpec((sides, TEAM * LINES, width), lambda t: (0, t, 0))


def pack_tokens(group_id, expert_ids, tokens, sides, expert_total):
    count, model_width = tokens.shape
    teams = expert_total // TEAM
    shape, spec = lines_out(sides, teams, model_width // CUT)
    return call(
        functools.partial(slots_kernel, expert_total),
        "pack_tokens",
        (shape, jax.ShapeDtypeStruct((2, count), jnp.int32)),
        grid=(teams,),
        in_specs=[pl.BlockSpec(memory_space=pltpu.HBM)] * 3,
        out_specs=(spec, whole((2, count))),
        scratch_shapes=[
            pltpu.VMEM((expert_total * CAP, model_width), BF16),
            pltpu.VMEM((TEAM * LINES, TEAM * LINES), BF16),
            pltpu.VMEM((1, count), jnp.int32),
            pltpu.VMEM((2, count), jnp.int32),
            pltpu.VMEM((count, model_width), BF16),
            pltpu.SemaphoreType.DMA((3,)),
        ],
    )(*(in_hbm(value) for value in (group_id[None], expert_ids.T, tokens)))


def grads_kernel(slot_ref, weight_ref, rows_ref, order_ref, out_ref, held):
    @pl.when(pl.program_id(0) == 0)
    def _():
        place = lax.broadcasted_iota(jnp.int32, (held.shape[0], slot_ref.shape[1]), 0)
        first, second = place == slot_ref[0:1, :], place == slot_ref[1:2, :]
        weight = jnp.where(first, weight_ref[0:1, :], 0.0)
        weight += jnp.where(second, weight_ref[1:2, :], 0.0)
        weight = jnp.sum(weight, axis=1, keepdims=True)
        picked = (first | second).astype(F32).astype(BF16)
        held[...] = (dot(picked, rows_ref[...]) * weight).astype(BF16)

    send_team(held, order_ref[...], out_ref)


def pack_grads(slot, weights, grad_out, order, sides, expert_total):
    count, model_width = grad_out.shape
    teams = expert_total // TEAM
    shape, spec = lines_out(sides, teams, model_width // CUT)
    return call(
        grads_kernel,
        "pack_grads",
        shape,
        grid=(teams,),
        in_specs=[
            whole((2, count)),
            whole((2, count)),
            whole(grad_out.shape),
            whole(order.shape),
        ],
        out_specs=spec,
        scratch_shapes=[pltpu.VMEM((expert_total * CAP, model_width), BF16)],
    )(slot, weights, grad_out, order)


def put_in_order(lines_ref, order_ref, rows_ref):
    width = lines_ref.shape[1]
    step, rows = TEAM * LINES, TEAM * CAP
    for t in range(lines_ref.shape[0] // step):
        moved = dot(order_ref[...], lines_ref[t * step : (t + 1) * step]).astype(BF16)
        for j in range(CUT):
            columns = slice(j * width, (j + 1) * width)
            rows_ref[t * rows : (t + 1) * rows, columns] = moved[j * rows : (j + 1) * rows]


def forward_kernel(
    lines_ref, order_ref, gate_ref, up_ref, down_ref, rows_ref, g_ref, u_ref, hidden_ref, *out_ref
):
    step = pl.program_id(0)
    width = lines_ref.shape[1]

    @pl.when(step == 0)
    def _():
        put_in_order(lines_ref, order_ref, rows_ref)
        g_ref[...] = jnp.zeros_like(g_ref)
        u_ref[...] = jnp.zeros_like(u_ref)

    rows = rows_ref[:, pl.ds(pl.multiple_of(step * width, width), width)]
    g_ref[...] += dot(rows, gate_ref[...])
    u_ref[...] += dot(rows, up_ref[...])

    @pl.when(step == pl.num_programs(0) - 1)
    def _():
        gate = g_ref[...]
        hidden = (gate * jax.nn.sigmoid(gate) * u_ref[...]).astype(BF16)
        hidden_ref[...] = hidden
        for ref in out_ref:
            for j in range(CUT):
                part = slice(j * width, (j + 1) * width)
                ref[:, part] = dot(hidden, down_ref[:, part]).astype(BF16)


def forward(lines, order, w_gate, w_up, w_down, own):
    width = lines.shape[1]
    half, model_width = lines.shape[0] // CUT, CUT * width
    units = w_down.shape[1]
    wide = jax.ShapeDtypeStruct((half, model_width), BF16)
    weight_spec = pl.BlockSpec((None, width, units), lambda k: (0, k, 0))
    act = whole((half, units))
    outs = [wide, pltpu.HBM((half, units), F32), pltpu.HBM((half, units), F32)]
    outs.append(jax.ShapeDtypeStruct((half, units), BF16))
    if not own:
        outs.append(wide)
    down_shape = (None, units, model_width if not own else width)
    return call(
        forward_kernel,
        "forward_own" if own else "forward_other",
        outs,
        BUSY,
        grid=(CUT,),
        in_specs=[
            whole(lines.shape),
            whole(order.shape),
            weight_spec,
            weight_spec,
            pl.BlockSpec(down_shape, lambda k: (0, 0, 0)),
        ],
        out_specs=[whole(wide.shape), act, act, act, whole(wide.shape)][: len(outs)],
    )(lines, order, w_gate, w_up, w_down)


def backward_kernel(
    lines_ref, order_ref, down_ref, g_ref, u_ref, gate_ref, up_ref, rows_ref, dg_ref, du_ref, *more
):
    step = pl.program_id(0)
    width = lines_ref.shape[1]
    *out_ref, total = more

    @pl.when(step == 0)
    def _():
        put_in_order(lines_ref, order_ref, rows_ref)
        total[...] = jnp.zeros_like(total)

    rows = rows_ref[:, pl.ds(pl.multiple_of(step * width, width), width)]
    total[...] += across(rows, down_ref[...])

    @pl.when(step == pl.num_programs(0) - 1)
    def _():
        gate, grad_hidden = g_ref[...], total[...]
        sigmoid_gate = jax.nn.sigmoid(gate)
        dg = grad_hidden * u_ref[...] * sigmoid_gate * (1.0 + gate * (1.0 - sigmoid_gate))
        dg = dg.astype(BF16)
        du = (grad_hidden * (gate * sigmoid_gate)).astype(BF16)
        dg_ref[...] = dg
        du_ref[...] = du
        for ref in out_ref:
            for j in range(CUT):
                part = slice(j * width, (j + 1) * width)
                ref[:, part] = (
                    across(dg, gate_ref[part, :]) + across(du, up_ref[part, :])
                ).astype(BF16)


def backward(lines, order, w_down, gate_pre, up_pre, w_gate, w_up, own):
    width = lines.shape[1]
    half, model_width = lines.shape[0] // CUT, CUT * width
    units = w_down.shape[1]
    wide = jax.ShapeDtypeStruct((half, model_width), BF16)
    weight_shape = (None, model_width if not own else units, units)
    weight_spec = pl.BlockSpec(weight_shape, lambda k: (0, 0, 0))
    act = whole((half, units))
    outs = [wide] + [jax.ShapeDtypeStruct((half, units), BF16)] * 2
    if not own:
        outs.append(wide)
    return call(
        backward_kernel,
        "backward_own" if own else "backward_other",
        outs,
        BUSY,
        grid=(CUT,),
        in_specs=[
            whole(lines.shape),
            whole(order.shape),
            pl.BlockSpec((None, units, width), lambda k: (0, 0, k)),
            act,
            act,
            weight_spec,
            weight_spec,
        ],
        out_specs=[whole(wide.shape), act, act, whole(wide.shape)][: len(outs)],
        scratch_shapes=[pltpu.VMEM((half, units), F32)],
    )(lines, order, w_down, in_hbm(gate_pre), in_hbm(up_pre), w_gate, w_up)


def out_kernel(hidden_ref, down_ref, total_ref):
    total_ref[...] = dot(hidden_ref[...], down_ref[...])


def product_out(hidden, w_down):
    half, units = hidden.shape
    model_width = w_down.shape[2]
    width = model_width // CUT
    return call(
        out_kernel,
        "product_out",
        jax.ShapeDtypeStruct((half, model_width), F32),
        BUSY,
        grid=(CUT,),
        in_specs=[
            whole((half, units)),
            pl.BlockSpec((None, units, width), lambda k: (0, 0, k)),
        ],
        out_specs=pl.BlockSpec((half, width), lambda k: (0, k)),
    )(hidden, w_down)


def in_kernel(dg_ref, du_ref, gate_ref, up_ref, total_ref):
    total_ref[...] = across(dg_ref[...], gate_ref[...]) + across(du_ref[...], up_ref[...])


def product_in(dg, du, w_gate, w_up):
    half, units = dg.shape
    model_width = w_gate.shape[1]
    width = model_width // CUT
    weight_spec = pl.BlockSpec((None, width, units), lambda k: (0, k, 0))
    return call(
        in_kernel,
        "product_in",
        jax.ShapeDtypeStruct((half, model_width), F32),
        BUSY,
        grid=(CUT,),
        in_specs=[whole((half, units)), whole((half, units)), weight_spec, weight_spec],
        out_specs=pl.BlockSpec((half, width), lambda k: (0, k)),
    )(dg, du, w_gate, w_up)


def lines_kernel(total_ref, arrived_ref, order_ref, out_ref):
    width = out_ref.shape[1]
    rows, step = TEAM * CAP, TEAM * LINES
    for t in range(total_ref.shape[0] // rows):
        team = slice(t * rows, (t + 1) * rows)
        pieces = []
        for j in range(CUT):
            part = slice(j * width, (j + 1) * width)
            pieces.append((total_ref[team, part] + arrived_ref[team, part].astype(F32)).astype(BF16))
        held = jnp.concatenate(pieces, axis=0)
        out_ref[t * step : (t + 1) * step, :] = dot(order_ref[...], held).astype(BF16)


def to_lines(total, arrived, order):
    half, model_width = total.shape
    width = model_width // CUT
    parts = 4
    rows = half // parts
    return call(
        lines_kernel,
        "to_lines",
        jax.ShapeDtypeStruct((half * CUT, width), BF16),
        grid=(parts,),
        in_specs=[
            pl.BlockSpec((rows, model_width), lambda k: (k, 0)),
            pl.BlockSpec((rows, model_width), lambda k: (k, 0)),
            whole(order.shape),
        ],
        out_specs=pl.BlockSpec((rows * CUT, width), lambda k: (k, 0)),
    )(total, arrived, order)


def columns_grad_kernel(own, other, dg_own, dg_other, du_own, du_other, gate_ref, up_ref):
    rows_own, rows_other = own[...].T, other[...].T
    gate_ref[...] = (dot(rows_own, dg_own[...]) + dot(rows_other, dg_other[...])).astype(BF16)
    up_ref[...] = (dot(rows_own, du_own[...]) + dot(rows_other, du_other[...])).astype(BF16)


def columns_grad(rows, dg, du):
    half, model_width = rows[0].shape
    units = dg[0].shape[1]
    piece = model_width // 8
    rows_spec = pl.BlockSpec((half, piece), lambda k: (0, k))
    out_spec = pl.BlockSpec((None, piece, units), lambda k: (0, k, 0))
    return call(
        columns_grad_kernel,
        "columns_grad",
        [jax.ShapeDtypeStruct((1, model_width, units), BF16)] * 2,
        grid=(model_width // piece,),
        in_specs=[rows_spec] * 2 + [whole((half, units))] * 4,
        out_specs=[out_spec] * 2,
    )(*rows, *dg, *du)


def rows_grad_kernel(hidden_own, hidden_other, own, other, down_ref):
    down_ref[...] = (
        dot(hidden_own[...].T, own[...]) + dot(hidden_other[...].T, other[...])
    ).astype(BF16)


def rows_grad(hidden, grads):
    half, model_width = grads[0].shape
    units = hidden[0].shape[1]
    piece = model_width // CUT
    rows_spec = pl.BlockSpec((half, piece), lambda k: (0, k))
    return call(
        rows_grad_kernel,
        "rows_grad",
        jax.ShapeDtypeStruct((1, units, model_width), BF16),
        grid=(CUT,),
        in_specs=[whole((half, units))] * 2 + [rows_spec] * 2,
        out_specs=pl.BlockSpec((None, units, piece), lambda k: (0, 0, k)),
    )(*hidden, *grads)


def both_chips(lines_ref):
    half = lines_ref.shape[0] // 2
    return (lines_ref[:half].astype(F32) + lines_ref[half:].astype(F32)).astype(BF16)


def mix_kernel(first_ref, second_ref, lines_ref, grad_ref, weight_ref, mixed_ref, score_ref):
    step = pl.program_id(0)
    count, piece = grad_ref.shape[0], lines_ref.shape[1]
    width = grad_ref.shape[1] // CUT

    @pl.when(step == 0)
    def _():
        score_ref[...] = jnp.zeros_like(score_ref)

    lines = both_chips(lines_ref)
    first = dot(first_ref[...], lines)
    second = dot(second_ref[...], lines)
    for j in range(CUT):
        rows = slice(j * count, (j + 1) * count)
        columns = pl.ds(pl.multiple_of(j * width + step * piece, piece), piece)
        grad = grad_ref[:, columns].astype(F32)
        mixed_ref[:, columns] = (
            weight_ref[:, 0:1] * first[rows] + weight_ref[:, 1:2] * second[rows]
        ).astype(BF16)
        score_ref[:, 0:1] += jnp.sum(grad * first[rows], axis=1, keepdims=True)
        score_ref[:, 1:2] += jnp.sum(grad * second[rows], axis=1, keepdims=True)


def mix(first, second, lines, grad_out, weights):
    total, width = lines.shape
    piece = width // CUT
    return call(
        mix_kernel,
        "mix",
        (
            jax.ShapeDtypeStruct(grad_out.shape, BF16),
            jax.ShapeDtypeStruct(weights.shape, F32),
        ),
        grid=(CUT,),
        in_specs=[
            whole(first.shape),
            whole(second.shape),
            pl.BlockSpec((total, piece), lambda n: (0, n)),
            whole(grad_out.shape),
            whole(weights.shape),
        ],
        out_specs=(whole(grad_out.shape), whole(weights.shape)),
    )(first, second, lines, grad_out, weights)


def unpack_kernel(either_ref, lines_ref, out_ref):
    step = pl.program_id(0)
    count, piece = out_ref.shape[0], lines_ref.shape[1]
    width = out_ref.shape[1] // CUT
    rows = dot(either_ref[...], both_chips(lines_ref)).astype(BF16)
    for j in range(CUT):
        columns = pl.ds(pl.multiple_of(j * width + step * piece, piece), piece)
        out_ref[:, columns] = rows[j * count : (j + 1) * count]


def unpack(either, lines, count):
    total, width = lines.shape
    piece = width // CUT
    return call(
        unpack_kernel,
        "unpack",
        jax.ShapeDtypeStruct((count, CUT * width), BF16),
        grid=(CUT,),
        in_specs=[whole(either.shape), pl.BlockSpec((total, piece), lambda n: (0, n))],
        out_specs=whole((count, CUT * width)),
    )(either, lines)


def body(tokens, grad_out, router_logits, group_id, expert_ids, w_gate, w_up, w_down):
    count = tokens.shape[0]
    expert_total = lax.axis_size(NODE)
    sides = lax.axis_size("h")
    order = order_matrix()
    to_travel, in_order = jnp.asarray(order), jnp.asarray(order.T)

    tokens_out, slot = pack_tokens(group_id, expert_ids, tokens, sides, expert_total)

    inside = group_id < expert_total // GSIZE
    chosen = group_id[:, None] * GSIZE + expert_ids
    weights, pull_back = jax.vjp(
        lambda values: gate_weights(values, group_id, chosen, inside), router_logits
    )
    grads_out = pack_grads(slot, weights.T, grad_out, to_travel, sides, expert_total)

    line = np.arange(expert_total * LINES)
    line_key = ((line // LINES * CAP + line % CAP) * CUT + line // CAP % CUT)[None, :]
    chunk = jnp.arange(CUT, dtype=jnp.int32)[:, None]

    def lines_of(slots):
        key = jnp.where(slots[None] >= 0, slots[None] * CUT + chunk, -1).reshape(CUT * count, 1)
        return key == line_key.astype(np.int32)

    first, second = lines_of(slot[0]), lines_of(slot[1])
    either = (first | second).astype(BF16)
    first, second = first.astype(BF16), second.astype(BF16)

    tokens_in, grads_out, first, second, either = lax.optimization_barrier(
        (exchange(tokens_out), grads_out, first, second, either)
    )
    grads_in = exchange(grads_out)
    lines_other = swap(tokens_in)
    weights3 = (w_gate, w_up, w_down)
    rows_own, gate_own, up_own, hidden_own = forward(tokens_in, in_order, *weights3, True)
    lines_other, hidden_own = lax.optimization_barrier((lines_other, hidden_own))
    rows_other, gate_other, up_other, hidden_other, out_other = forward(
        lines_other, in_order, *weights3, False
    )
    out_lines = to_lines(product_out(hidden_own, w_down), swap(out_other), to_travel)
    out_lines, grads_in = lax.optimization_barrier((out_lines, grads_in))
    out_back = exchange(out_lines)

    lines_other = swap(grads_in)
    grads_own, dg_own, du_own = backward(
        grads_in, in_order, w_down, gate_own, up_own, w_gate, w_up, True
    )
    lines_other, dg_own, du_own = lax.optimization_barrier((lines_other, dg_own, du_own))
    grads_other, dg_other, du_other, in_other = backward(
        lines_other, in_order, w_down, gate_other, up_other, w_gate, w_up, False
    )
    in_lines = to_lines(product_in(dg_own, du_own, w_gate, w_up), swap(in_other), to_travel)
    in_lines, out_back, rows, grads, hidden, dg, du = lax.optimization_barrier(
        (
            in_lines,
            out_back,
            (rows_own, rows_other),
            (grads_own, grads_other),
            (hidden_own, hidden_other),
            (dg_own, dg_other),
            (du_own, du_other),
        )
    )
    in_back = exchange(in_lines)

    grad_gate, grad_up = columns_grad(rows, dg, du)
    grad_down = rows_grad(hidden, grads)
    mixed, scores = mix(first, second, out_back, grad_out, weights)
    d_logits = pull_back(scores)[0]
    d_tokens = unpack(either, in_back, count)
    return (mixed, d_tokens, d_logits, grad_gate, grad_up, grad_down)


def solution(mesh):
    fine = Mesh(mesh.devices.reshape(4, 4, 2, 2, 2), ALL)
    return jax.shard_map(
        body,
        mesh=fine,
        in_specs=(
            P(ALL, None),
            P(ALL, None),
            P(ALL, None),
            P(ALL),
            P(ALL, None),
            P(NODE, None, LOCAL),
            P(NODE, None, LOCAL),
            P(NODE, LOCAL, None),
        ),
        out_specs=(
            P(ALL, None),
            P(ALL, None),
            P(ALL, None),
            P(NODE, None, LOCAL),
            P(NODE, None, LOCAL),
            P(NODE, LOCAL, None),
        ),
        check_vma=False,
    )
```

```python
import functools

import jax
import jax.numpy as jnp
import numpy as np
from jax import lax
from jax.experimental import pallas as pl
from jax.experimental.pallas import tpu as pltpu
from jax.sharding import Mesh, PartitionSpec as P

GSIZE = 8
CAP = 6
CUT = 4
TEAM = 8
LINES = CUT * CAP
BUSY = 200_000_000_000
ALL = ("y", "x", "l", "h", "c")
NODE = ("y", "x", "l")
LOCAL = ("h", "c")
F32 = jnp.float32
BF16 = jnp.bfloat16


def dot(a, b, dims=((1,), (0,))):
    return lax.dot_general(a, b, (dims, ((), ())), preferred_element_type=F32)


def across(a, b):
    return dot(a, b, ((1,), (1,)))


def call(kernel, name, outs, flops=1, **more):
    return pl.pallas_call(
        kernel,
        out_shape=outs,
        name=name,
        cost_estimate=pl.CostEstimate(flops=flops, bytes_accessed=1, transcendentals=0),
        compiler_params=pltpu.CompilerParams(vmem_limit_bytes=52 << 20),
        **more,
    )


def in_hbm(value):
    return pltpu.with_memory_space_constraint(value, pltpu.HBM)


def whole(shape):
    return pl.BlockSpec(shape, lambda *_: (0,) * len(shape))


def gate_weights(logits, group_ids, chosen, inside):
    probabilities = jax.nn.softmax(logits, axis=-1)
    columns = jnp.arange(logits.shape[1], dtype=jnp.int32)
    member = ((columns // GSIZE)[None, :] == group_ids[:, None]).astype(logits.dtype)
    group_mass = jnp.sum(probabilities * member, axis=1)
    picked = jnp.sum(
        jnp.where(chosen[:, :, None] == columns[None, None, :], logits[:, None, :], 0.0), axis=2
    )
    pair_share = jax.nn.softmax(picked, axis=-1)
    return jnp.where(inside[:, None], group_mass[:, None] * pair_share, 0.0)


def half_turn():
    ys, xs, ls = (lax.axis_size(name) for name in NODE)
    return ((ys // 2) * xs + xs // 2) * ls


def peer_groups():
    ys, xs, ls, hs, cores = (lax.axis_size(name) for name in ALL)
    experts = ys * xs * ls
    return [
        [(((e ^ (half_turn() * c)) * hs) + (h ^ c)) * cores + c for h in range(hs) for e in range(experts)]
        for c in range(cores)
    ]


def exchange(value):
    blocks = value.reshape(-1, LINES, value.shape[-1])
    out = lax.all_to_all(
        blocks, ALL, split_axis=0, concat_axis=0, axis_index_groups=peer_groups(), tiled=True
    )
    return out.reshape(-1, value.shape[-1])


def swap(value):
    return lax.ppermute(value, "c", [(0, 1), (1, 0)])


def order_matrix():
    line = np.arange(TEAM * LINES)
    member, chunk, slot = line // LINES, line // CAP % CUT, line % CAP
    wanted = (chunk * TEAM + member) * CAP + slot
    return (wanted[:, None] == line[None, :]).astype(BF16)


def gathered(ref, start, width):
    team = pl.ds(start, TEAM * CAP)
    return jnp.concatenate([ref[team, j * width : (j + 1) * width] for j in range(CUT)], axis=0)


def order_in_kernel(shape):
    line = lax.broadcasted_iota(jnp.int32, (shape[0], 1), 0)
    member, chunk, slot = line // LINES, line // CAP % CUT, line % CAP
    wanted = (chunk * TEAM + member) * CAP + slot
    return (wanted == lax.broadcasted_iota(jnp.int32, shape, 1)).astype(F32).astype(BF16)


def send_team(held, order, out_ref):
    team, width = pl.program_id(0), out_ref.shape[2]
    start = pl.multiple_of(team * (TEAM * CAP), 16)
    lines = dot(order, gathered(held, start, width)).astype(BF16)
    for side in range(out_ref.shape[0]):
        out_ref[side] = lines


def slots_kernel(expert_total, group_in, expert_in, rows_in, out_ref, slot_ref, held, order, *own):
    group_ref, expert_ref, rows_ref, sems = own

    @pl.when(pl.program_id(0) == 0)
    def _():
        pairs = ((group_in, group_ref), (expert_in, expert_ref), (rows_in, rows_ref))
        copies = [
            pltpu.make_async_copy(src, dst, sems.at[k]) for k, (src, dst) in enumerate(pairs)
        ]
        for copy in copies:
            copy.start()
        order[...] = order_in_kernel(order.shape)
        copies[0].wait()
        copies[1].wait()
        count = group_ref.shape[1]
        group = group_ref[...]
        inside = group < expert_total // GSIZE
        turn = half_turn() * lax.axis_index("c")
        down = lax.broadcasted_iota(jnp.int32, (count, count), 0)
        along = lax.broadcasted_iota(jnp.int32, (count, count), 1)
        expert = lax.broadcasted_iota(jnp.int32, (expert_total, count), 0)
        targets, hots = [], []
        for k in range(2):
            place = (group * GSIZE + expert_ref[k : k + 1, :]) ^ turn
            target = jnp.where(inside, place, expert_total)
            targets.append(target)
            hots.append((expert == target).astype(F32))
        before = (down < along).astype(F32).astype(BF16)
        earlier = dot((hots[0] + hots[1]).astype(BF16), before)
        place = lax.broadcasted_iota(jnp.int32, (expert_total * CAP, count), 0)
        picked = None
        for k in range(2):
            rank = jnp.sum(hots[k] * earlier, axis=0, keepdims=True).astype(jnp.int32)
            slot = jnp.where(inside, targets[k] * CAP + rank, -1)
            slot_ref[k : k + 1, :] = slot
            match = place == slot
            picked = match if picked is None else picked | match
        picked = picked.astype(F32).astype(BF16)
        copies[2].wait()
        held[...] = dot(picked, rows_ref[...]).astype(BF16)

    send_team(held, order[...], out_ref)


def lines_out(sides, teams, width):
    shape = jax.ShapeDtypeStruct((sides, teams * TEAM * LINES, width), BF16)
    return shape, pl.BlockSpec((sides, TEAM * LINES, width), lambda t: (0, t, 0))


def pack_tokens(group_id, expert_ids, tokens, sides, expert_total):
    count, model_width = tokens.shape
    teams = expert_total // TEAM
    shape, spec = lines_out(sides, teams, model_width // CUT)
    return call(
        functools.partial(slots_kernel, expert_total),
        "pack_tokens",
        (shape, jax.ShapeDtypeStruct((2, count), jnp.int32)),
        grid=(teams,),
        in_specs=[pl.BlockSpec(memory_space=pltpu.HBM)] * 3,
        out_specs=(spec, whole((2, count))),
        scratch_shapes=[
            pltpu.VMEM((expert_total * CAP, model_width), BF16),
            pltpu.VMEM((TEAM * LINES, TEAM * LINES), BF16),
            pltpu.VMEM((1, count), jnp.int32),
            pltpu.VMEM((2, count), jnp.int32),
            pltpu.VMEM((count, model_width), BF16),
            pltpu.SemaphoreType.DMA((3,)),
        ],
    )(*(in_hbm(value) for value in (group_id[None], expert_ids.T, tokens)))


def grads_kernel(slot_ref, weight_ref, rows_ref, order_ref, out_ref, held):
    @pl.when(pl.program_id(0) == 0)
    def _():
        place = lax.broadcasted_iota(jnp.int32, (held.shape[0], slot_ref.shape[1]), 0)
        first, second = place == slot_ref[0:1, :], place == slot_ref[1:2, :]
        weight = jnp.where(first, weight_ref[0:1, :], 0.0)
        weight += jnp.where(second, weight_ref[1:2, :], 0.0)
        weight = jnp.sum(weight, axis=1, keepdims=True)
        picked = (first | second).astype(F32).astype(BF16)
        held[...] = (dot(picked, rows_ref[...]) * weight).astype(BF16)

    send_team(held, order_ref[...], out_ref)


def pack_grads(slot, weights, grad_out, order, sides, expert_total):
    count, model_width = grad_out.shape
    teams = expert_total // TEAM
    shape, spec = lines_out(sides, teams, model_width // CUT)
    return call(
        grads_kernel,
        "pack_grads",
        shape,
        grid=(teams,),
        in_specs=[
            whole((2, count)),
            whole((2, count)),
            whole(grad_out.shape),
            whole(order.shape),
        ],
        out_specs=spec,
        scratch_shapes=[pltpu.VMEM((expert_total * CAP, model_width), BF16)],
    )(slot, weights, grad_out, order)


def put_in_order(lines_ref, order_ref, rows_ref):
    width = lines_ref.shape[1]
    step, rows = TEAM * LINES, TEAM * CAP
    for t in range(lines_ref.shape[0] // step):
        moved = dot(order_ref[...], lines_ref[t * step : (t + 1) * step]).astype(BF16)
        for j in range(CUT):
            columns = slice(j * width, (j + 1) * width)
            rows_ref[t * rows : (t + 1) * rows, columns] = moved[j * rows : (j + 1) * rows]


def forward_kernel(
    lines_ref, order_ref, gate_ref, up_ref, down_ref, rows_ref, g_ref, u_ref, hidden_ref, *out_ref
):
    step = pl.program_id(0)
    width = lines_ref.shape[1]

    @pl.when(step == 0)
    def _():
        put_in_order(lines_ref, order_ref, rows_ref)
        g_ref[...] = jnp.zeros_like(g_ref)
        u_ref[...] = jnp.zeros_like(u_ref)

    rows = rows_ref[:, pl.ds(pl.multiple_of(step * width, width), width)]
    g_ref[...] += dot(rows, gate_ref[...])
    u_ref[...] += dot(rows, up_ref[...])

    @pl.when(step == pl.num_programs(0) - 1)
    def _():
        gate = g_ref[...]
        hidden = (gate * jax.nn.sigmoid(gate) * u_ref[...]).astype(BF16)
        hidden_ref[...] = hidden
        for ref in out_ref:
            for j in range(CUT):
                part = slice(j * width, (j + 1) * width)
                ref[:, part] = dot(hidden, down_ref[:, part]).astype(BF16)


def forward(lines, order, w_gate, w_up, w_down, own):
    width = lines.shape[1]
    half, model_width = lines.shape[0] // CUT, CUT * width
    units = w_down.shape[1]
    wide = jax.ShapeDtypeStruct((half, model_width), BF16)
    weight_spec = pl.BlockSpec((None, width, units), lambda k: (0, k, 0))
    act = whole((half, units))
    outs = [wide, pltpu.HBM((half, units), F32), pltpu.HBM((half, units), F32)]
    outs.append(jax.ShapeDtypeStruct((half, units), BF16))
    if not own:
        outs.append(wide)
    down_shape = (None, units, model_width if not own else width)
    return call(
        forward_kernel,
        "forward_own" if own else "forward_other",
        outs,
        BUSY,
        grid=(CUT,),
        in_specs=[
            whole(lines.shape),
            whole(order.shape),
            weight_spec,
            weight_spec,
            pl.BlockSpec(down_shape, lambda k: (0, 0, 0)),
        ],
        out_specs=[whole(wide.shape), act, act, act, whole(wide.shape)][: len(outs)],
    )(lines, order, w_gate, w_up, w_down)


def backward_kernel(
    lines_ref, order_ref, down_ref, g_ref, u_ref, gate_ref, up_ref, rows_ref, dg_ref, du_ref, *more
):
    step = pl.program_id(0)
    width = lines_ref.shape[1]
    *out_ref, total = more

    @pl.when(step == 0)
    def _():
        put_in_order(lines_ref, order_ref, rows_ref)
        total[...] = jnp.zeros_like(total)

    rows = rows_ref[:, pl.ds(pl.multiple_of(step * width, width), width)]
    total[...] += across(rows, down_ref[...])

    @pl.when(step == pl.num_programs(0) - 1)
    def _():
        gate, grad_hidden = g_ref[...], total[...]
        sigmoid_gate = jax.nn.sigmoid(gate)
        dg = grad_hidden * u_ref[...] * sigmoid_gate * (1.0 + gate * (1.0 - sigmoid_gate))
        dg = dg.astype(BF16)
        du = (grad_hidden * (gate * sigmoid_gate)).astype(BF16)
        dg_ref[...] = dg
        du_ref[...] = du
        for ref in out_ref:
            for j in range(CUT):
                part = slice(j * width, (j + 1) * width)
                ref[:, part] = (
                    across(dg, gate_ref[part, :]) + across(du, up_ref[part, :])
                ).astype(BF16)


def backward(lines, order, w_down, gate_pre, up_pre, w_gate, w_up, own):
    width = lines.shape[1]
    half, model_width = lines.shape[0] // CUT, CUT * width
    units = w_down.shape[1]
    wide = jax.ShapeDtypeStruct((half, model_width), BF16)
    weight_shape = (None, model_width if not own else units, units)
    weight_spec = pl.BlockSpec(weight_shape, lambda k: (0, 0, 0))
    act = whole((half, units))
    outs = [wide] + [jax.ShapeDtypeStruct((half, units), BF16)] * 2
    if not own:
        outs.append(wide)
    return call(
        backward_kernel,
        "backward_own" if own else "backward_other",
        outs,
        BUSY,
        grid=(CUT,),
        in_specs=[
            whole(lines.shape),
            whole(order.shape),
            pl.BlockSpec((None, units, width), lambda k: (0, 0, k)),
            act,
            act,
            weight_spec,
            weight_spec,
        ],
        out_specs=[whole(wide.shape), act, act, whole(wide.shape)][: len(outs)],
        scratch_shapes=[pltpu.VMEM((half, units), F32)],
    )(lines, order, w_down, in_hbm(gate_pre), in_hbm(up_pre), w_gate, w_up)


def out_kernel(hidden_ref, down_ref, total_ref):
    total_ref[...] = dot(hidden_ref[...], down_ref[...])


def product_out(hidden, w_down):
    half, units = hidden.shape
    model_width = w_down.shape[2]
    width = model_width // CUT
    return call(
        out_kernel,
        "product_out",
        jax.ShapeDtypeStruct((half, model_width), F32),
        BUSY,
        grid=(CUT,),
        in_specs=[
            whole((half, units)),
            pl.BlockSpec((None, units, width), lambda k: (0, 0, k)),
        ],
        out_specs=pl.BlockSpec((half, width), lambda k: (0, k)),
    )(hidden, w_down)


def in_kernel(dg_ref, du_ref, gate_ref, up_ref, total_ref):
    total_ref[...] = across(dg_ref[...], gate_ref[...]) + across(du_ref[...], up_ref[...])


def product_in(dg, du, w_gate, w_up):
    half, units = dg.shape
    model_width = w_gate.shape[1]
    width = model_width // CUT
    weight_spec = pl.BlockSpec((None, width, units), lambda k: (0, k, 0))
    return call(
        in_kernel,
        "product_in",
        jax.ShapeDtypeStruct((half, model_width), F32),
        BUSY,
        grid=(CUT,),
        in_specs=[whole((half, units)), whole((half, units)), weight_spec, weight_spec],
        out_specs=pl.BlockSpec((half, width), lambda k: (0, k)),
    )(dg, du, w_gate, w_up)


def lines_kernel(total_ref, arrived_ref, order_ref, out_ref):
    width = out_ref.shape[1]
    rows, step = TEAM * CAP, TEAM * LINES
    for t in range(total_ref.shape[0] // rows):
        team = slice(t * rows, (t + 1) * rows)
        pieces = []
        for j in range(CUT):
            part = slice(j * width, (j + 1) * width)
            pieces.append((total_ref[team, part] + arrived_ref[team, part].astype(F32)).astype(BF16))
        held = jnp.concatenate(pieces, axis=0)
        out_ref[t * step : (t + 1) * step, :] = dot(order_ref[...], held).astype(BF16)


def to_lines(total, arrived, order):
    half, model_width = total.shape
    width = model_width // CUT
    parts = 4
    rows = half // parts
    return call(
        lines_kernel,
        "to_lines",
        jax.ShapeDtypeStruct((half * CUT, width), BF16),
        grid=(parts,),
        in_specs=[
            pl.BlockSpec((rows, model_width), lambda k: (k, 0)),
            pl.BlockSpec((rows, model_width), lambda k: (k, 0)),
            whole(order.shape),
        ],
        out_specs=pl.BlockSpec((rows * CUT, width), lambda k: (k, 0)),
    )(total, arrived, order)


def columns_grad_kernel(own, other, dg_own, dg_other, du_own, du_other, gate_ref, up_ref):
    rows_own, rows_other = own[...].T, other[...].T
    gate_ref[...] = (dot(rows_own, dg_own[...]) + dot(rows_other, dg_other[...])).astype(BF16)
    up_ref[...] = (dot(rows_own, du_own[...]) + dot(rows_other, du_other[...])).astype(BF16)


def columns_grad(rows, dg, du):
    half, model_width = rows[0].shape
    units = dg[0].shape[1]
    piece = model_width // 8
    rows_spec = pl.BlockSpec((half, piece), lambda k: (0, k))
    out_spec = pl.BlockSpec((None, piece, units), lambda k: (0, k, 0))
    return call(
        columns_grad_kernel,
        "columns_grad",
        [jax.ShapeDtypeStruct((1, model_width, units), BF16)] * 2,
        grid=(model_width // piece,),
        in_specs=[rows_spec] * 2 + [whole((half, units))] * 4,
        out_specs=[out_spec] * 2,
    )(*rows, *dg, *du)


def rows_grad_kernel(hidden_own, hidden_other, own, other, down_ref):
    down_ref[...] = (
        dot(hidden_own[...].T, own[...]) + dot(hidden_other[...].T, other[...])
    ).astype(BF16)


def rows_grad(hidden, grads):
    half, model_width = grads[0].shape
    units = hidden[0].shape[1]
    piece = model_width // CUT
    rows_spec = pl.BlockSpec((half, piece), lambda k: (0, k))
    return call(
        rows_grad_kernel,
        "rows_grad",
        jax.ShapeDtypeStruct((1, units, model_width), BF16),
        grid=(CUT,),
        in_specs=[whole((half, units))] * 2 + [rows_spec] * 2,
        out_specs=pl.BlockSpec((None, units, piece), lambda k: (0, 0, k)),
    )(*hidden, *grads)


def both_chips(lines_ref):
    half = lines_ref.shape[0] // 2
    return (lines_ref[:half].astype(F32) + lines_ref[half:].astype(F32)).astype(BF16)


def mix_kernel(first_ref, second_ref, lines_ref, grad_ref, weight_ref, mixed_ref, score_ref):
    step = pl.program_id(0)
    count, piece = grad_ref.shape[0], lines_ref.shape[1]
    width = grad_ref.shape[1] // CUT

    @pl.when(step == 0)
    def _():
        score_ref[...] = jnp.zeros_like(score_ref)

    lines = both_chips(lines_ref)
    first = dot(first_ref[...], lines)
    second = dot(second_ref[...], lines)
    for j in range(CUT):
        rows = slice(j * count, (j + 1) * count)
        columns = pl.ds(pl.multiple_of(j * width + step * piece, piece), piece)
        grad = grad_ref[:, columns].astype(F32)
        mixed_ref[:, columns] = (
            weight_ref[:, 0:1] * first[rows] + weight_ref[:, 1:2] * second[rows]
        ).astype(BF16)
        score_ref[:, 0:1] += jnp.sum(grad * first[rows], axis=1, keepdims=True)
        score_ref[:, 1:2] += jnp.sum(grad * second[rows], axis=1, keepdims=True)


def mix(first, second, lines, grad_out, weights):
    total, width = lines.shape
    piece = width // CUT
    return call(
        mix_kernel,
        "mix",
        (
            jax.ShapeDtypeStruct(grad_out.shape, BF16),
            jax.ShapeDtypeStruct(weights.shape, F32),
        ),
        grid=(CUT,),
        in_specs=[
            whole(first.shape),
            whole(second.shape),
            pl.BlockSpec((total, piece), lambda n: (0, n)),
            whole(grad_out.shape),
            whole(weights.shape),
        ],
        out_specs=(whole(grad_out.shape), whole(weights.shape)),
    )(first, second, lines, grad_out, weights)


def unpack_kernel(either_ref, lines_ref, out_ref):
    step = pl.program_id(0)
    count, piece = out_ref.shape[0], lines_ref.shape[1]
    width = out_ref.shape[1] // CUT
    rows = dot(either_ref[...], both_chips(lines_ref)).astype(BF16)
    for j in range(CUT):
        columns = pl.ds(pl.multiple_of(j * width + step * piece, piece), piece)
        out_ref[:, columns] = rows[j * count : (j + 1) * count]


def unpack(either, lines, count):
    total, width = lines.shape
    piece = width // CUT
    return call(
        unpack_kernel,
        "unpack",
        jax.ShapeDtypeStruct((count, CUT * width), BF16),
        grid=(CUT,),
        in_specs=[whole(either.shape), pl.BlockSpec((total, piece), lambda n: (0, n))],
        out_specs=whole((count, CUT * width)),
    )(either, lines)


def body(tokens, grad_out, router_logits, group_id, expert_ids, w_gate, w_up, w_down):
    count = tokens.shape[0]
    expert_total = lax.axis_size(NODE)
    sides = lax.axis_size("h")
    order = order_matrix()
    to_travel, in_order = jnp.asarray(order), jnp.asarray(order.T)

    tokens_out, slot = pack_tokens(group_id, expert_ids, tokens, sides, expert_total)

    inside = group_id < expert_total // GSIZE
    chosen = group_id[:, None] * GSIZE + expert_ids
    weights, pull_back = jax.vjp(
        lambda values: gate_weights(values, group_id, chosen, inside), router_logits
    )
    grads_out = pack_grads(slot, weights.T, grad_out, to_travel, sides, expert_total)

    line = np.arange(expert_total * LINES)
    line_key = ((line // LINES * CAP + line % CAP) * CUT + line // CAP % CUT)[None, :]
    chunk = jnp.arange(CUT, dtype=jnp.int32)[:, None]

    def lines_of(slots):
        key = jnp.where(slots[None] >= 0, slots[None] * CUT + chunk, -1).reshape(CUT * count, 1)
        return key == line_key.astype(np.int32)

    first, second = lines_of(slot[0]), lines_of(slot[1])
    either = (first | second).astype(BF16)
    first, second = first.astype(BF16), second.astype(BF16)

    tokens_in, grads_out, first, second, either = lax.optimization_barrier(
        (exchange(tokens_out), grads_out, first, second, either)
    )
    grads_in = exchange(grads_out)
    lines_other = swap(tokens_in)
    weights3 = (w_gate, w_up, w_down)
    rows_own, gate_own, up_own, hidden_own = forward(tokens_in, in_order, *weights3, True)
    lines_other, hidden_own = lax.optimization_barrier((lines_other, hidden_own))
    rows_other, gate_other, up_other, hidden_other, out_other = forward(
        lines_other, in_order, *weights3, False
    )
    out_lines = to_lines(product_out(hidden_own, w_down), swap(out_other), to_travel)
    out_lines, grads_in = lax.optimization_barrier((out_lines, grads_in))
    out_back = exchange(out_lines)

    lines_other = swap(grads_in)
    grads_own, dg_own, du_own = backward(
        grads_in, in_order, w_down, gate_own, up_own, w_gate, w_up, True
    )
    lines_other, dg_own, du_own = lax.optimization_barrier((lines_other, dg_own, du_own))
    grads_other, dg_other, du_other, in_other = backward(
        lines_other, in_order, w_down, gate_other, up_other, w_gate, w_up, False
    )
    in_lines = to_lines(product_in(dg_own, du_own, w_gate, w_up), swap(in_other), to_travel)
    in_lines, out_back, rows, grads, hidden, dg, du = lax.optimization_barrier(
        (
            in_lines,
            out_back,
            (rows_own, rows_other),
            (grads_own, grads_other),
            (hidden_own, hidden_other),
            (dg_own, dg_other),
            (du_own, du_other),
        )
    )
    in_back = exchange(in_lines)

    grad_gate, grad_up = columns_grad(rows, dg, du)
    grad_down = rows_grad(hidden, grads)
    mixed, scores = mix(first, second, out_back, grad_out, weights)
    d_logits = pull_back(scores)[0]
    d_tokens = unpack(either, in_back, count)
    return (mixed, d_tokens, d_logits, grad_gate, grad_up, grad_down)


def solution(mesh):
    fine = Mesh(mesh.devices.reshape(4, 4, 2, 2, 2), ALL)
    return jax.shard_map(
        body,
        mesh=fine,
        in_specs=(
            P(ALL, None),
            P(ALL, None),
            P(ALL, None),
            P(ALL),
            P(ALL, None),
            P(NODE, None, LOCAL),
            P(NODE, None, LOCAL),
            P(NODE, LOCAL, None),
        ),
        out_specs=(
            P(ALL, None),
            P(ALL, None),
            P(ALL, None),
            P(NODE, None, LOCAL),
            P(NODE, None, LOCAL),
            P(NODE, LOCAL, None),
        ),
        check_vma=False,
    )
```

```python
import functools

import jax
import jax.numpy as jnp
import numpy as np
from jax import lax
from jax.experimental import pallas as pl
from jax.experimental.pallas import tpu as pltpu
from jax.sharding import Mesh, PartitionSpec as P

GSIZE = 8
CAP = 6
CUT = 4
TEAM = 8
LINES = CUT * CAP
BUSY = 200_000_000_000
ALL = ("y", "x", "l", "h", "c")
NODE = ("y", "x", "l")
LOCAL = ("h", "c")
F32 = jnp.float32
BF16 = jnp.bfloat16


def dot(a, b, dims=((1,), (0,))):
    return lax.dot_general(a, b, (dims, ((), ())), preferred_element_type=F32)


def across(a, b):
    return dot(a, b, ((1,), (1,)))


def call(kernel, name, outs, flops=1, **more):
    return pl.pallas_call(
        kernel,
        out_shape=outs,
        name=name,
        cost_estimate=pl.CostEstimate(flops=flops, bytes_accessed=1, transcendentals=0),
        compiler_params=pltpu.CompilerParams(vmem_limit_bytes=52 << 20),
        **more,
    )


def in_hbm(value):
    return pltpu.with_memory_space_constraint(value, pltpu.HBM)


def whole(shape):
    return pl.BlockSpec(shape, lambda *_: (0,) * len(shape))


def gate_weights(logits, group_ids, chosen, inside):
    probabilities = jax.nn.softmax(logits, axis=-1)
    columns = jnp.arange(logits.shape[1], dtype=jnp.int32)
    member = ((columns // GSIZE)[None, :] == group_ids[:, None]).astype(logits.dtype)
    group_mass = jnp.sum(probabilities * member, axis=1)
    picked = jnp.sum(
        jnp.where(chosen[:, :, None] == columns[None, None, :], logits[:, None, :], 0.0), axis=2
    )
    pair_share = jax.nn.softmax(picked, axis=-1)
    return jnp.where(inside[:, None], group_mass[:, None] * pair_share, 0.0)


def half_turn():
    ys, xs, ls = (lax.axis_size(name) for name in NODE)
    return ((ys // 2) * xs + xs // 2) * ls


def peer_groups():
    ys, xs, ls, hs, cores = (lax.axis_size(name) for name in ALL)
    experts = ys * xs * ls
    return [
        [(((e ^ (half_turn() * c)) * hs) + (h ^ c)) * cores + c for h in range(hs) for e in range(experts)]
        for c in range(cores)
    ]


def exchange(value):
    blocks = value.reshape(-1, LINES, value.shape[-1])
    out = lax.all_to_all(
        blocks, ALL, split_axis=0, concat_axis=0, axis_index_groups=peer_groups(), tiled=True
    )
    return out.reshape(-1, value.shape[-1])


def swap(value):
    return lax.ppermute(value, "c", [(0, 1), (1, 0)])


def order_matrix():
    line = np.arange(TEAM * LINES)
    member, chunk, slot = line // LINES, line // CAP % CUT, line % CAP
    wanted = (chunk * TEAM + member) * CAP + slot
    return (wanted[:, None] == line[None, :]).astype(BF16)


def gathered(ref, start, width):
    team = pl.ds(start, TEAM * CAP)
    return jnp.concatenate([ref[team, j * width : (j + 1) * width] for j in range(CUT)], axis=0)


def order_in_kernel(shape):
    line = lax.broadcasted_iota(jnp.int32, (shape[0], 1), 0)
    member, chunk, slot = line // LINES, line // CAP % CUT, line % CAP
    wanted = (chunk * TEAM + member) * CAP + slot
    return (wanted == lax.broadcasted_iota(jnp.int32, shape, 1)).astype(F32).astype(BF16)


def send_team(held, order, out_ref):
    team, width = pl.program_id(0), out_ref.shape[2]
    start = pl.multiple_of(team * (TEAM * CAP), 16)
    lines = dot(order, gathered(held, start, width)).astype(BF16)
    for side in range(out_ref.shape[0]):
        out_ref[side] = lines


def slots_kernel(expert_total, group_in, expert_in, rows_in, out_ref, slot_ref, held, order, *own):
    group_ref, expert_ref, rows_ref, sems = own

    @pl.when(pl.program_id(0) == 0)
    def _():
        pairs = ((group_in, group_ref), (expert_in, expert_ref), (rows_in, rows_ref))
        copies = [
            pltpu.make_async_copy(src, dst, sems.at[k]) for k, (src, dst) in enumerate(pairs)
        ]
        for copy in copies:
            copy.start()
        order[...] = order_in_kernel(order.shape)
        copies[0].wait()
        copies[1].wait()
        count = group_ref.shape[1]
        group = group_ref[...]
        inside = group < expert_total // GSIZE
        turn = half_turn() * lax.axis_index("c")
        down = lax.broadcasted_iota(jnp.int32, (count, count), 0)
        along = lax.broadcasted_iota(jnp.int32, (count, count), 1)
        expert = lax.broadcasted_iota(jnp.int32, (expert_total, count), 0)
        targets, hots = [], []
        for k in range(2):
            place = (group * GSIZE + expert_ref[k : k + 1, :]) ^ turn
            target = jnp.where(inside, place, expert_total)
            targets.append(target)
            hots.append((expert == target).astype(F32))
        before = (down < along).astype(F32).astype(BF16)
        earlier = dot((hots[0] + hots[1]).astype(BF16), before)
        place = lax.broadcasted_iota(jnp.int32, (expert_total * CAP, count), 0)
        picked = None
        for k in range(2):
            rank = jnp.sum(hots[k] * earlier, axis=0, keepdims=True).astype(jnp.int32)
            slot = jnp.where(inside, targets[k] * CAP + rank, -1)
            slot_ref[k : k + 1, :] = slot
            match = place == slot
            picked = match if picked is None else picked | match
        picked = picked.astype(F32).astype(BF16)
        copies[2].wait()
        held[...] = dot(picked, rows_ref[...]).astype(BF16)

    send_team(held, order[...], out_ref)


def lines_out(sides, teams, width):
    shape = jax.ShapeDtypeStruct((sides, teams * TEAM * LINES, width), BF16)
    return shape, pl.BlockSpec((sides, TEAM * LINES, width), lambda t: (0, t, 0))


def pack_tokens(group_id, expert_ids, tokens, sides, expert_total):
    count, model_width = tokens.shape
    teams = expert_total // TEAM
    shape, spec = lines_out(sides, teams, model_width // CUT)
    return call(
        functools.partial(slots_kernel, expert_total),
        "pack_tokens",
        (shape, jax.ShapeDtypeStruct((2, count), jnp.int32)),
        grid=(teams,),
        in_specs=[pl.BlockSpec(memory_space=pltpu.HBM)] * 3,
        out_specs=(spec, whole((2, count))),
        scratch_shapes=[
            pltpu.VMEM((expert_total * CAP, model_width), BF16),
            pltpu.VMEM((TEAM * LINES, TEAM * LINES), BF16),
            pltpu.VMEM((1, count), jnp.int32),
            pltpu.VMEM((2, count), jnp.int32),
            pltpu.VMEM((count, model_width), BF16),
            pltpu.SemaphoreType.DMA((3,)),
        ],
    )(*(in_hbm(value) for value in (group_id[None], expert_ids.T, tokens)))


def grads_kernel(slot_ref, weight_ref, rows_ref, order_ref, out_ref, held):
    @pl.when(pl.program_id(0) == 0)
    def _():
        place = lax.broadcasted_iota(jnp.int32, (held.shape[0], slot_ref.shape[1]), 0)
        first, second = place == slot_ref[0:1, :], place == slot_ref[1:2, :]
        weight = jnp.where(first, weight_ref[0:1, :], 0.0)
        weight += jnp.where(second, weight_ref[1:2, :], 0.0)
        weight = jnp.sum(weight, axis=1, keepdims=True)
        picked = (first | second).astype(F32).astype(BF16)
        held[...] = (dot(picked, rows_ref[...]) * weight).astype(BF16)

    send_team(held, order_ref[...], out_ref)


def pack_grads(slot, weights, grad_out, order, sides, expert_total):
    count, model_width = grad_out.shape
    teams = expert_total // TEAM
    shape, spec = lines_out(sides, teams, model_width // CUT)
    return call(
        grads_kernel,
        "pack_grads",
        shape,
        grid=(teams,),
        in_specs=[
            whole((2, count)),
            whole((2, count)),
            whole(grad_out.shape),
            whole(order.shape),
        ],
        out_specs=spec,
        scratch_shapes=[pltpu.VMEM((expert_total * CAP, model_width), BF16)],
    )(slot, weights, grad_out, order)


def put_in_order(lines_ref, order_ref, rows_ref):
    width = lines_ref.shape[1]
    step, rows = TEAM * LINES, TEAM * CAP
    for t in range(lines_ref.shape[0] // step):
        moved = dot(order_ref[...], lines_ref[t * step : (t + 1) * step]).astype(BF16)
        for j in range(CUT):
            columns = slice(j * width, (j + 1) * width)
            rows_ref[t * rows : (t + 1) * rows, columns] = moved[j * rows : (j + 1) * rows]


def forward_kernel(
    lines_ref, order_ref, gate_ref, up_ref, down_ref, rows_ref, g_ref, u_ref, hidden_ref, *out_ref
):
    step = pl.program_id(0)
    width = lines_ref.shape[1]

    @pl.when(step == 0)
    def _():
        put_in_order(lines_ref, order_ref, rows_ref)
        g_ref[...] = jnp.zeros_like(g_ref)
        u_ref[...] = jnp.zeros_like(u_ref)

    rows = rows_ref[:, pl.ds(pl.multiple_of(step * width, width), width)]
    g_ref[...] += dot(rows, gate_ref[...])
    u_ref[...] += dot(rows, up_ref[...])

    @pl.when(step == pl.num_programs(0) - 1)
    def _():
        gate = g_ref[...]
        hidden = (gate * jax.nn.sigmoid(gate) * u_ref[...]).astype(BF16)
        hidden_ref[...] = hidden
        for ref in out_ref:
            for j in range(CUT):
                part = slice(j * width, (j + 1) * width)
                ref[:, part] = dot(hidden, down_ref[:, part]).astype(BF16)


def forward(lines, order, w_gate, w_up, w_down, own):
    width = lines.shape[1]
    half, model_width = lines.shape[0] // CUT, CUT * width
    units = w_down.shape[1]
    wide = jax.ShapeDtypeStruct((half, model_width), BF16)
    weight_spec = pl.BlockSpec((None, width, units), lambda k: (0, k, 0))
    act = whole((half, units))
    outs = [wide, pltpu.HBM((half, units), F32), pltpu.HBM((half, units), F32)]
    outs.append(jax.ShapeDtypeStruct((half, units), BF16))
    if not own:
        outs.append(wide)
    down_shape = (None, units, model_width if not own else width)
    return call(
        forward_kernel,
        "forward_own" if own else "forward_other",
        outs,
        BUSY,
        grid=(CUT,),
        in_specs=[
            whole(lines.shape),
            whole(order.shape),
            weight_spec,
            weight_spec,
            pl.BlockSpec(down_shape, lambda k: (0, 0, 0)),
        ],
        out_specs=[whole(wide.shape), act, act, act, whole(wide.shape)][: len(outs)],
    )(lines, order, w_gate, w_up, w_down)


def backward_kernel(
    lines_ref, order_ref, down_ref, g_ref, u_ref, gate_ref, up_ref, rows_ref, dg_ref, du_ref, *more
):
    step = pl.program_id(0)
    width = lines_ref.shape[1]
    *out_ref, total = more

    @pl.when(step == 0)
    def _():
        put_in_order(lines_ref, order_ref, rows_ref)
        total[...] = jnp.zeros_like(total)

    rows = rows_ref[:, pl.ds(pl.multiple_of(step * width, width), width)]
    total[...] += across(rows, down_ref[...])

    @pl.when(step == pl.num_programs(0) - 1)
    def _():
        gate, grad_hidden = g_ref[...], total[...]
        sigmoid_gate = jax.nn.sigmoid(gate)
        dg = grad_hidden * u_ref[...] * sigmoid_gate * (1.0 + gate * (1.0 - sigmoid_gate))
        dg = dg.astype(BF16)
        du = (grad_hidden * (gate * sigmoid_gate)).astype(BF16)
        dg_ref[...] = dg
        du_ref[...] = du
        for ref in out_ref:
            for j in range(CUT):
                part = slice(j * width, (j + 1) * width)
                ref[:, part] = (
                    across(dg, gate_ref[part, :]) + across(du, up_ref[part, :])
                ).astype(BF16)


def backward(lines, order, w_down, gate_pre, up_pre, w_gate, w_up, own):
    width = lines.shape[1]
    half, model_width = lines.shape[0] // CUT, CUT * width
    units = w_down.shape[1]
    wide = jax.ShapeDtypeStruct((half, model_width), BF16)
    weight_shape = (None, model_width if not own else units, units)
    weight_spec = pl.BlockSpec(weight_shape, lambda k: (0, 0, 0))
    act = whole((half, units))
    outs = [wide] + [jax.ShapeDtypeStruct((half, units), BF16)] * 2
    if not own:
        outs.append(wide)
    return call(
        backward_kernel,
        "backward_own" if own else "backward_other",
        outs,
        BUSY,
        grid=(CUT,),
        in_specs=[
            whole(lines.shape),
            whole(order.shape),
            pl.BlockSpec((None, units, width), lambda k: (0, 0, k)),
            act,
            act,
            weight_spec,
            weight_spec,
        ],
        out_specs=[whole(wide.shape), act, act, whole(wide.shape)][: len(outs)],
        scratch_shapes=[pltpu.VMEM((half, units), F32)],
    )(lines, order, w_down, in_hbm(gate_pre), in_hbm(up_pre), w_gate, w_up)


def out_kernel(hidden_ref, down_ref, total_ref):
    total_ref[...] = dot(hidden_ref[...], down_ref[...]).astype(BF16)


def product_out(hidden, w_down):
    half, units = hidden.shape
    model_width = w_down.shape[2]
    width = model_width // CUT
    return call(
        out_kernel,
        "product_out",
        jax.ShapeDtypeStruct((half, model_width), BF16),
        BUSY,
        grid=(CUT,),
        in_specs=[
            whole((half, units)),
            pl.BlockSpec((None, units, width), lambda k: (0, 0, k)),
        ],
        out_specs=pl.BlockSpec((half, width), lambda k: (0, k)),
    )(hidden, w_down)


def in_kernel(dg_ref, du_ref, gate_ref, up_ref, total_ref):
    total_ref[...] = (
        across(dg_ref[...], gate_ref[...]) + across(du_ref[...], up_ref[...])
    ).astype(BF16)


def product_in(dg, du, w_gate, w_up):
    half, units = dg.shape
    model_width = w_gate.shape[1]
    width = model_width // CUT
    weight_spec = pl.BlockSpec((None, width, units), lambda k: (0, k, 0))
    return call(
        in_kernel,
        "product_in",
        jax.ShapeDtypeStruct((half, model_width), BF16),
        BUSY,
        grid=(CUT,),
        in_specs=[whole((half, units)), whole((half, units)), weight_spec, weight_spec],
        out_specs=pl.BlockSpec((half, width), lambda k: (0, k)),
    )(dg, du, w_gate, w_up)


def lines_kernel(total_ref, arrived_ref, order_ref, out_ref):
    width = out_ref.shape[1]
    rows, step = TEAM * CAP, TEAM * LINES
    for t in range(total_ref.shape[0] // rows):
        team = slice(t * rows, (t + 1) * rows)
        pieces = []
        for j in range(CUT):
            part = slice(j * width, (j + 1) * width)
            both = total_ref[team, part].astype(F32) + arrived_ref[team, part].astype(F32)
            pieces.append(both.astype(BF16))
        held = jnp.concatenate(pieces, axis=0)
        out_ref[t * step : (t + 1) * step, :] = dot(order_ref[...], held).astype(BF16)


def to_lines(total, arrived, order):
    half, model_width = total.shape
    width = model_width // CUT
    parts = 4
    rows = half // parts
    return call(
        lines_kernel,
        "to_lines",
        jax.ShapeDtypeStruct((half * CUT, width), BF16),
        grid=(parts,),
        in_specs=[
            pl.BlockSpec((rows, model_width), lambda k: (k, 0)),
            pl.BlockSpec((rows, model_width), lambda k: (k, 0)),
            whole(order.shape),
        ],
        out_specs=pl.BlockSpec((rows * CUT, width), lambda k: (k, 0)),
    )(total, arrived, order)


def columns_grad_kernel(own, other, dg_own, dg_other, du_own, du_other, gate_ref, up_ref):
    rows_own, rows_other = own[...].T, other[...].T
    gate_ref[...] = (dot(rows_own, dg_own[...]) + dot(rows_other, dg_other[...])).astype(BF16)
    up_ref[...] = (dot(rows_own, du_own[...]) + dot(rows_other, du_other[...])).astype(BF16)


def columns_grad(rows, dg, du):
    half, model_width = rows[0].shape
    units = dg[0].shape[1]
    piece = model_width // 8
    rows_spec = pl.BlockSpec((half, piece), lambda k: (0, k))
    out_spec = pl.BlockSpec((None, piece, units), lambda k: (0, k, 0))
    return call(
        columns_grad_kernel,
        "columns_grad",
        [jax.ShapeDtypeStruct((1, model_width, units), BF16)] * 2,
        grid=(model_width // piece,),
        in_specs=[rows_spec] * 2 + [whole((half, units))] * 4,
        out_specs=[out_spec] * 2,
    )(*rows, *dg, *du)


def rows_grad_kernel(hidden_own, hidden_other, own, other, down_ref):
    down_ref[...] = (
        dot(hidden_own[...].T, own[...]) + dot(hidden_other[...].T, other[...])
    ).astype(BF16)


def rows_grad(hidden, grads):
    half, model_width = grads[0].shape
    units = hidden[0].shape[1]
    piece = model_width // CUT
    rows_spec = pl.BlockSpec((half, piece), lambda k: (0, k))
    return call(
        rows_grad_kernel,
        "rows_grad",
        jax.ShapeDtypeStruct((1, units, model_width), BF16),
        grid=(CUT,),
        in_specs=[whole((half, units))] * 2 + [rows_spec] * 2,
        out_specs=pl.BlockSpec((None, units, piece), lambda k: (0, 0, k)),
    )(*hidden, *grads)


def both_chips(lines_ref):
    half = lines_ref.shape[0] // 2
    return (lines_ref[:half].astype(F32) + lines_ref[half:].astype(F32)).astype(BF16)


def mix_kernel(first_ref, second_ref, lines_ref, grad_ref, weight_ref, mixed_ref, score_ref):
    step = pl.program_id(0)
    count, piece = grad_ref.shape[0], lines_ref.shape[1]
    width = grad_ref.shape[1] // CUT

    @pl.when(step == 0)
    def _():
        score_ref[...] = jnp.zeros_like(score_ref)

    lines = both_chips(lines_ref)
    first = dot(first_ref[...], lines)
    second = dot(second_ref[...], lines)
    for j in range(CUT):
        rows = slice(j * count, (j + 1) * count)
        columns = pl.ds(pl.multiple_of(j * width + step * piece, piece), piece)
        grad = grad_ref[:, columns].astype(F32)
        mixed_ref[:, columns] = (
            weight_ref[:, 0:1] * first[rows] + weight_ref[:, 1:2] * second[rows]
        ).astype(BF16)
        score_ref[:, 0:1] += jnp.sum(grad * first[rows], axis=1, keepdims=True)
        score_ref[:, 1:2] += jnp.sum(grad * second[rows], axis=1, keepdims=True)


def mix(first, second, lines, grad_out, weights):
    total, width = lines.shape
    piece = width // CUT
    return call(
        mix_kernel,
        "mix",
        (
            jax.ShapeDtypeStruct(grad_out.shape, BF16),
            jax.ShapeDtypeStruct(weights.shape, F32),
        ),
        grid=(CUT,),
        in_specs=[
            whole(first.shape),
            whole(second.shape),
            pl.BlockSpec((total, piece), lambda n: (0, n)),
            whole(grad_out.shape),
            whole(weights.shape),
        ],
        out_specs=(whole(grad_out.shape), whole(weights.shape)),
    )(first, second, lines, grad_out, weights)


def unpack_kernel(either_ref, lines_ref, out_ref):
    step = pl.program_id(0)
    count, piece = out_ref.shape[0], lines_ref.shape[1]
    width = out_ref.shape[1] // CUT
    rows = dot(either_ref[...], both_chips(lines_ref)).astype(BF16)
    for j in range(CUT):
        columns = pl.ds(pl.multiple_of(j * width + step * piece, piece), piece)
        out_ref[:, columns] = rows[j * count : (j + 1) * count]


def unpack(either, lines, count):
    total, width = lines.shape
    piece = width // CUT
    return call(
        unpack_kernel,
        "unpack",
        jax.ShapeDtypeStruct((count, CUT * width), BF16),
        grid=(CUT,),
        in_specs=[whole(either.shape), pl.BlockSpec((total, piece), lambda n: (0, n))],
        out_specs=whole((count, CUT * width)),
    )(either, lines)


def body(tokens, grad_out, router_logits, group_id, expert_ids, w_gate, w_up, w_down):
    count = tokens.shape[0]
    expert_total = lax.axis_size(NODE)
    sides = lax.axis_size("h")
    order = order_matrix()
    to_travel, in_order = jnp.asarray(order), jnp.asarray(order.T)

    tokens_out, slot = pack_tokens(group_id, expert_ids, tokens, sides, expert_total)

    inside = group_id < expert_total // GSIZE
    chosen = group_id[:, None] * GSIZE + expert_ids
    weights, pull_back = jax.vjp(
        lambda values: gate_weights(values, group_id, chosen, inside), router_logits
    )
    grads_out = pack_grads(slot, weights.T, grad_out, to_travel, sides, expert_total)

    line = np.arange(expert_total * LINES)
    line_key = ((line // LINES * CAP + line % CAP) * CUT + line // CAP % CUT)[None, :]
    chunk = jnp.arange(CUT, dtype=jnp.int32)[:, None]

    def lines_of(slots):
        key = jnp.where(slots[None] >= 0, slots[None] * CUT + chunk, -1).reshape(CUT * count, 1)
        return key == line_key.astype(np.int32)

    first, second = lines_of(slot[0]), lines_of(slot[1])
    either = (first | second).astype(BF16)
    first, second = first.astype(BF16), second.astype(BF16)

    tokens_in, grads_out, first, second, either = lax.optimization_barrier(
        (exchange(tokens_out), grads_out, first, second, either)
    )
    grads_in = exchange(grads_out)
    lines_other = swap(tokens_in)
    weights3 = (w_gate, w_up, w_down)
    rows_own, gate_own, up_own, hidden_own = forward(tokens_in, in_order, *weights3, True)
    lines_other, hidden_own = lax.optimization_barrier((lines_other, hidden_own))
    rows_other, gate_other, up_other, hidden_other, out_other = forward(
        lines_other, in_order, *weights3, False
    )
    out_lines = to_lines(product_out(hidden_own, w_down), swap(out_other), to_travel)
    out_lines, grads_in = lax.optimization_barrier((out_lines, grads_in))
    out_back = exchange(out_lines)

    lines_other = swap(grads_in)
    grads_own, dg_own, du_own = backward(
        grads_in, in_order, w_down, gate_own, up_own, w_gate, w_up, True
    )
    lines_other, dg_own, du_own = lax.optimization_barrier((lines_other, dg_own, du_own))
    grads_other, dg_other, du_other, in_other = backward(
        lines_other, in_order, w_down, gate_other, up_other, w_gate, w_up, False
    )
    in_lines = to_lines(product_in(dg_own, du_own, w_gate, w_up), swap(in_other), to_travel)
    in_lines, out_back, rows, grads, hidden, dg, du = lax.optimization_barrier(
        (
            in_lines,
            out_back,
            (rows_own, rows_other),
            (grads_own, grads_other),
            (hidden_own, hidden_other),
            (dg_own, dg_other),
            (du_own, du_other),
        )
    )
    in_back = exchange(in_lines)

    grad_gate, grad_up = columns_grad(rows, dg, du)
    grad_down = rows_grad(hidden, grads)
    mixed, scores = mix(first, second, out_back, grad_out, weights)
    d_logits = pull_back(scores)[0]
    d_tokens = unpack(either, in_back, count)
    return (mixed, d_tokens, d_logits, grad_gate, grad_up, grad_down)


def solution(mesh):
    fine = Mesh(mesh.devices.reshape(4, 4, 2, 2, 2), ALL)
    return jax.shard_map(
        body,
        mesh=fine,
        in_specs=(
            P(ALL, None),
            P(ALL, None),
            P(ALL, None),
            P(ALL),
            P(ALL, None),
            P(NODE, None, LOCAL),
            P(NODE, None, LOCAL),
            P(NODE, LOCAL, None),
        ),
        out_specs=(
            P(ALL, None),
            P(ALL, None),
            P(ALL, None),
            P(NODE, None, LOCAL),
            P(NODE, None, LOCAL),
            P(NODE, LOCAL, None),
        ),
        check_vma=False,
    )
```
